512 devices in a mesh: section: 8 (over z_lo, core), table: 64 (over x, y, z_hi).
Axes of the slice: x: 4, y: 8, z: 8 (z_hi: 2, z_lo: 4; z = z_hi * 4 + z_lo), core: 2. Of those that a mesh axis runs over, the one named last changes fastest.
Arguments:
- gate_a: bfloat16 [8, 4096, 4096], P('section', 'table'), may hold values from -6 to 6
- cotangent_a: bfloat16 [8, 4096, 4096], P('section', 'table'), may hold values from -6 to 6
- gate_b: bfloat16 [8, 4096, 4096], P('section', 'table'), may hold values from -6 to 6
- table: bfloat16 [4096, 4096], P('table'), may hold values from -6 to 6
- row_ids: int32 [8, 2, 64, 128], P('section', None, 'table'), may hold values from 0 to 4095, as said below
- slots: int32 [8, 2, 4096, 128], P('section', None, 'table'), may hold values from 0 to 127, as said below
- weights: float32 [8, 2, 4096, 128], P('section', None, 'table'), may hold values from 0.02 to 0.2
Outputs:
- mixed_b: bfloat16 [8, 4096, 4096], P('section', 'table')
- grad_gate_a: bfloat16 [8, 4096, 4096], P('section', 'table')
- grad_weights_a: float32 [8, 4096, 128], P('section', 'table')
- grad_table: float32 [4096, 4096], P('table', 'section')
The draws below stay inside these ranges and needn't reach their ends.
Inputs may be any that keep to these rules, and one draw needn't show every extreme that they name: `row_ids`: row r is held by index r // 64 of table. The 128 ids of one list are distinct, and at most 8 of them are held by one index of table; in every section and micro-batch some index of table holds 8 ids of every device's list. `slots`: the 32 picks of one token and head are distinct, and every position of a device's list is picked by some token of that device and micro-batch.
All inputs are finite; a program needn't handle non-finite values.
Results may differ from the reference program's by a relative error of at most 0.0057.
Values may be sent and summed in bfloat16 or wider, within the bound.
No kernel may reach another device: no remote copies, remote signals or barrier semaphores. Data moves between devices by JAX's collectives and lax.ppermute only.
A program may use at most 128 MiB of HBM per device.

```python
import math
import jax
import jax.numpy as jnp
from jax import lax

D = 4096
HEADS = 4
TOPK = 32
TOK_DEV = 64
ROWS_DEV = 64
USED = 128
ROW_LIMIT = 8
PICKS = 128
TOKENS = 4096
ROWS = 4096
N_SECTION = 8
N_TABLE = 64


def owner_rows(table_group, device_key):
    popular_key, boost_key = jax.random.split(table_group)
    hottest = jax.random.randint(popular_key, (), 0, N_TABLE)
    score_boost = jax.random.randint(boost_key, (N_TABLE,), 0, 4) * 8192
    scoring_key, key_order, key_shuffle = jax.random.split(device_key, 3)
    row_scores = jax.random.randint(scoring_key, (N_TABLE, ROW_LIMIT), 0, 16384) + score_boost[:, None]
    owner_ids = jnp.arange(N_TABLE, dtype=jnp.int32)
    row_scores = jnp.where(owner_ids[:, None] == hottest, 1 << 17, row_scores)
    ranked = row_scores.reshape(-1) * (N_TABLE * ROW_LIMIT) + jnp.arange(N_TABLE * ROW_LIMIT, dtype=jnp.int32)
    _, chosen = lax.top_k(ranked, USED)
    owner_of = chosen // ROW_LIMIT
    column = chosen % ROW_LIMIT
    order_keys = jax.random.randint(key_order, (N_TABLE, ROWS_DEV), 0, 1 << 16) * ROWS_DEV + jnp.arange(ROWS_DEV, dtype=jnp.int32)[None, :]
    shuffled = jnp.argsort(order_keys, axis=1)
    within = shuffled[owner_of, column]
    listed = owner_of * ROWS_DEV + within
    return listed[jax.random.permutation(key_shuffle, USED)]


def draw_row_ids(key, part):

    def group_lists(index):
        table_group = jax.random.fold_in(key, 7000 + index)

        def one_device(device):
            return owner_rows(table_group, jax.random.fold_in(table_group, 100 + device))
        return jax.vmap(one_device)(jnp.arange(N_TABLE))
    lists = jax.vmap(group_lists)(jnp.arange(N_SECTION * 2))
    return lists.reshape(N_SECTION, 2, N_TABLE, USED).astype(jnp.int32)


def slot_block(block_key):
    key_pairs, key_slots, scoring_key = jax.random.split(block_key, 3)
    pair_rank = jnp.argsort(jax.random.permutation(key_pairs, TOK_DEV * HEADS))
    slot_rank = jnp.argsort(jax.random.permutation(key_slots, USED))
    row_scores = jax.random.randint(scoring_key, (TOK_DEV * HEADS, USED), 0, 1 << 16)
    forced = pair_rank[:, None] == (slot_rank // TOPK)[None, :]
    row_scores = jnp.where(forced, 1 << 17, row_scores)
    ranked = row_scores * USED + jnp.arange(USED, dtype=jnp.int32)[None, :]
    _, picked = lax.top_k(ranked, TOPK)
    return picked.reshape(TOK_DEV, PICKS).astype(jnp.int32)


def draw_slots(key, part):

    def one_block(index):
        return slot_block(jax.random.fold_in(key, 9000 + index))
    blocks = jax.vmap(one_block)(jnp.arange(N_SECTION * 2 * N_TABLE))
    return blocks.reshape(N_SECTION, 2, N_TABLE * TOK_DEV, PICKS)


def level_of(rng, dims, pieces, least, largest):
    level, own = 1.0, jax.random.fold_in(rng, 6)
    for axis_at, shards_of in pieces:
        draws = jnp.exp(jax.random.uniform(jax.random.fold_in(own, axis_at), (shards_of,), jnp.float32, least / len(pieces), largest / len(pieces)))
        level = level * jnp.repeat(draws, dims[axis_at] // shards_of).reshape([-1 if axis == axis_at else 1 for axis in range(len(dims))])
    return level


def scatter_about(rng, extent, scale, most, cuts=(), held_as=jnp.bfloat16):
    gain = level_of(rng, extent, cuts, -0.22, 0.18) if cuts else 1.0
    result = jax.random.normal(rng, extent, jnp.float32) * scale * gain
    return jnp.minimum(jnp.maximum(result, -most), most).astype(held_as)


def setup_inputs(seed: int = 0) -> dict:
    splits = jax.random.split(jax.random.key(seed), 8)
    return {
        "gate_a": scatter_about(splits[0], (N_SECTION, TOKENS, D), 1.0, 6.0, ((0, 8), (1, 64))),
        "cotangent_a": scatter_about(splits[1], (N_SECTION, TOKENS, D), 1.0, 6.0, ((0, 8), (1, 64))),
        "gate_b": scatter_about(splits[2], (N_SECTION, TOKENS, D), 1.0, 6.0, ((0, 8), (1, 64))),
        "table": scatter_about(splits[3], (ROWS, D), 1.0, 6.0, ((0, 64),)),
        "row_ids": draw_row_ids(jax.random.fold_in(splits[7], 71), 0),
        "slots": draw_slots(jax.random.fold_in(splits[7], 71), 0),
        "weights": jnp.clip(jnp.exp(math.log(0.2) - 2.3025851 * jax.random.uniform(splits[6], (N_SECTION, 2, TOKENS, PICKS), jnp.float32) ** level_of(splits[6], (N_SECTION, 2, TOKENS, PICKS), ((0, 8), (2, 64)), -0.2, 0.2)), 0.02, 0.2),
    }


def combine_table(slot_rows, weight_rows, listed):
    matches = slot_rows[:, :, None] == jnp.arange(listed, dtype=jnp.int32)[None, None, :]
    return jnp.sum(jnp.where(matches, weight_rows[:, :, None], jnp.zeros_like(weight_rows[:, :, None])), axis=1).astype(jnp.bfloat16)


def reference(gate_a, cotangent_a, gate_b, table, row_ids, slots, weights):
    section_count = gate_a.shape[0]
    tokens = gate_a.shape[1] // N_TABLE
    features = table.shape[1]

    def split_tokens(values):
        return values.reshape((section_count * N_TABLE, tokens) + values.shape[2:])

    def split_micro(values):
        values = values.reshape(section_count, 2, N_TABLE, tokens, values.shape[-1])
        return jnp.transpose(values, (0, 2, 1, 3, 4)).reshape(section_count * N_TABLE, 2, tokens, values.shape[-1])

    id_lists = jnp.transpose(row_ids, (0, 2, 1, 3)).reshape(section_count * N_TABLE, 2, USED)

    def device_step(grad_table, inputs):
        gate_one, cotangent_one, gate_two, list_pair, slot_pair, weight_pair = inputs
        fetched_a = jnp.take(table, list_pair[0], axis=0)
        fetched_b = jnp.take(table, list_pair[1], axis=0)
        mixing_a = combine_table(slot_pair[0], weight_pair[0], USED)
        mixing_b = combine_table(slot_pair[1], weight_pair[1], USED)
        memory_b = jnp.dot(mixing_b, fetched_b, preferred_element_type=jnp.float32)
        gate_value = gate_two.astype(jnp.float32)
        mixed = (gate_value * jax.nn.sigmoid(gate_value) * memory_b).astype(jnp.bfloat16)
        memory_a = jnp.dot(mixing_a, fetched_a, preferred_element_type=jnp.float32)
        gate_value = gate_one.astype(jnp.float32)
        incoming = cotangent_one.astype(jnp.float32)
        logistic = jax.nn.sigmoid(gate_value)
        grad_gate = (incoming * memory_a * logistic * (1.0 + gate_value * (1.0 - logistic))).astype(jnp.bfloat16)
        grad_memory = (incoming * gate_value * logistic).astype(jnp.bfloat16)
        row_scores = lax.dot_general(grad_memory, fetched_a, (((1,), (1,)), ((), ())), preferred_element_type=jnp.float32)
        grad_weights = jnp.take_along_axis(row_scores, slot_pair[0], axis=1)
        grad_rows = lax.dot_general(mixing_a, grad_memory, (((0,), (0,)), ((), ())), preferred_element_type=jnp.float32).astype(jnp.bfloat16)
        grad_table = grad_table.at[list_pair[0]].add(grad_rows.astype(jnp.float32))
        return grad_table, (mixed, grad_gate, grad_weights)

    inputs = (split_tokens(gate_a), split_tokens(cotangent_a), split_tokens(gate_b), id_lists, split_micro(slots), split_micro(weights))
    grad_table, outputs = lax.scan(device_step, jnp.zeros(table.shape, jnp.float32), inputs)
    mixed, grad_gate, grad_weights = outputs
    mixed = mixed.reshape(section_count, N_TABLE * tokens, features)
    grad_gate = grad_gate.reshape(section_count, N_TABLE * tokens, features)
    grad_weights = grad_weights.reshape(section_count, N_TABLE * tokens, grad_weights.shape[-1])
    return mixed, grad_gate, grad_weights, grad_table
```

```python
import jax
import jax.numpy as jnp
from jax import lax
from jax.experimental import pallas as pl
from jax.experimental.pallas import tpu as pltpu
from jax.sharding import Mesh
from jax.sharding import PartitionSpec as P

SECTION = ("zl1", "zl0", "c")
TABLE = ("x1", "x0", "y1", "y0", "zh")
GRAD_GROUP = ("x1", "zl0", "c", "x0", "y0")
ROW_GROUP = ("x1", "zl0", "c", "x0")
RING = ("y1", "y0")
ROWS_DEV = 64
F32 = jnp.float32
BF16 = jnp.bfloat16
VMEM = pltpu.CompilerParams(vmem_limit_bytes=40 * 1024 * 1024)


def mixing_of(slots, weights, listed):
    matches = slots[:, :, None] == jnp.arange(listed, dtype=jnp.int32)[None, None, :]
    return jnp.sum(jnp.where(matches, weights[:, :, None], 0.0), axis=1).astype(BF16)


def gated(gate, incoming):
    g = gate.astype(F32)
    sig = 1.0 / (1.0 + jnp.exp(-g))
    return g, sig, incoming.astype(F32)


def outgoing_kernel(gate_ref, cot_ref, mix_ref, ids_ref, out_ref):
    g, sig, inc = gated(gate_ref[...], cot_ref[...])
    grad_memory = (inc * g * sig).astype(BF16)
    rows = lax.dot_general(
        mix_ref[...], grad_memory, (((0,), (0,)), ((), ())), preferred_element_type=F32
    ).astype(BF16)
    listed = rows.shape[0]
    for k in range(out_ref.shape[0]):
        out_ref[k, :listed, :] = rows[:, k * 128 : (k + 1) * 128]
        out_ref[k, listed:, :] = ids_ref[...]


def outgoing(gate, cot, mixing, id_rows, features):
    tokens, width = gate.shape
    listed = mixing.shape[1]
    chunks, step = width // features, 4
    return pl.pallas_call(
        outgoing_kernel,
        grid=(chunks // step,),
        in_specs=[
            pl.BlockSpec((tokens, step * features), lambda i: (0, i)),
            pl.BlockSpec((tokens, step * features), lambda i: (0, i)),
            pl.BlockSpec((tokens, listed), lambda i: (0, 0)),
            pl.BlockSpec((16, listed), lambda i: (0, 0)),
        ],
        out_specs=pl.BlockSpec((step, listed + 16, features), lambda i: (i, 0, 0)),
        out_shape=jax.ShapeDtypeStruct((chunks, listed + 16, features), BF16),
        compiler_params=VMEM,
        name="outgoing_rows",
    )(gate, cot, mixing, id_rows)


def dense_kernel(ids_ref, rows_ref, out_ref):
    tile, features = out_ref.shape
    lists, listed = ids_ref.shape
    row = (lax.broadcasted_iota(jnp.int32, (tile, listed), 0) + pl.program_id(0) * tile).astype(F32)
    total = jnp.zeros((tile, features), F32)
    together = 8
    for first in range(0, lists, together):
        hot = [
            jnp.where(row == ids_ref[pl.ds(k, 1), :], 1.0, 0.0).astype(BF16)
            for k in range(first, first + together)
        ]
        rows = [rows_ref[k, :listed, :] for k in range(first, first + together)]
        total += jnp.dot(
            jnp.concatenate(hot, axis=1), jnp.concatenate(rows, axis=0), preferred_element_type=F32
        )
    out_ref[...] = total.astype(BF16)


def dense_rows(ids, received, rows):
    lists, listed = ids.shape
    features = received.shape[-1]
    tile = 256
    return pl.pallas_call(
        dense_kernel,
        grid=(rows // tile,),
        in_specs=[
            pl.BlockSpec((lists, listed), lambda i: (0, 0)),
            pl.BlockSpec(received.shape, lambda i: (0, 0, 0)),
        ],
        out_specs=pl.BlockSpec((tile, features), lambda i: (i, 0)),
        out_shape=jax.ShapeDtypeStruct((rows, features), BF16),
        compiler_params=VMEM,
        name="dense_rows",
    )(ids, received)


def pick_kernel(ids_ref, place_ref, *refs):
    blocks, out_ref = refs[:-1], refs[-1]
    lists, listed = ids_ref.shape[1:]
    wanted = jnp.concatenate(
        [jnp.transpose(jnp.broadcast_to(ids_ref[0, k : k + 1, :], (128, listed))) for k in range(lists)],
        axis=0,
    )
    total = jnp.zeros(out_ref.shape[1:], F32)
    for b, block in enumerate(blocks):
        rows = block.shape[0]
        hot = [
            jnp.where(wanted == place_ref[b : b + 1, q : q + 128], 1.0, 0.0).astype(BF16)
            for q in range(0, rows, 128)
        ]
        total += jnp.dot(jnp.concatenate(hot, axis=1), block[...], preferred_element_type=F32)
    out_ref[0] = total.astype(BF16)


def picked_rows(ids, places, blocks):
    members, lists, listed = ids.shape
    rows, features = blocks[0].shape
    return pl.pallas_call(
        pick_kernel,
        grid=(members,),
        in_specs=[
            pl.BlockSpec((1, lists, listed), lambda i: (i, 0, 0)),
            pl.BlockSpec(places.shape, lambda i: (0, 0)),
        ]
        + [pl.BlockSpec((rows, features), lambda i: (0, 0))] * len(blocks),
        out_specs=pl.BlockSpec((1, lists * listed, features), lambda i: (i, 0, 0)),
        out_shape=jax.ShapeDtypeStruct((members, lists * listed, features), BF16),
        compiler_params=VMEM,
        name="picked_rows",
    )(ids, places, *blocks)


def final_kernel(
    rows_ref, mix_a_ref, mix_b_ref, gate_a_ref, cot_ref, gate_b_ref, slots_ref,
    mixed_ref, grad_gate_ref, grad_weights_ref, scores_ref,
):
    listed = mix_a_ref.shape[1]
    fetched_a = rows_ref[0, :listed, :]
    fetched_b = rows_ref[0, listed:, :]
    memory_b = jnp.dot(mix_b_ref[...], fetched_b, preferred_element_type=F32)
    gb = gate_b_ref[...].astype(F32)
    mixed_ref[...] = (gb / (1.0 + jnp.exp(-gb)) * memory_b).astype(BF16)
    memory_a = jnp.dot(mix_a_ref[...], fetched_a, preferred_element_type=F32)
    g, sig, inc = gated(gate_a_ref[...], cot_ref[...])
    grad_gate_ref[...] = (inc * memory_a * sig * (1.0 + g * (1.0 - sig))).astype(BF16)
    grad_memory = (inc * g * sig).astype(BF16)
    part = lax.dot_general(
        grad_memory, fetched_a, (((1,), (1,)), ((), ())), preferred_element_type=F32
    )

    @pl.when(pl.program_id(0) == 0)
    def _():
        scores_ref[...] = part

    @pl.when(pl.program_id(0) > 0)
    def _():
        scores_ref[...] += part

    @pl.when(pl.program_id(0) == pl.num_programs(0) - 1)
    def _():
        grad_weights_ref[...] = jnp.take_along_axis(scores_ref[...], slots_ref[...], axis=1)


def final_outputs(fetched, mix_a, mix_b, gate_a, cot, gate_b, slots_a):
    chunks, rows, features = fetched.shape
    tokens, width = gate_a.shape
    listed = mix_a.shape[1]
    whole = pl.BlockSpec((tokens, listed), lambda i: (0, 0))
    part = pl.BlockSpec((tokens, features), lambda i: (0, i))
    return pl.pallas_call(
        final_kernel,
        grid=(chunks,),
        in_specs=[
            pl.BlockSpec((1, rows, features), lambda i: (i, 0, 0)),
            whole, whole, part, part, part, whole,
        ],
        out_specs=[part, part, whole],
        out_shape=[
            jax.ShapeDtypeStruct((tokens, width), BF16),
            jax.ShapeDtypeStruct((tokens, width), BF16),
            jax.ShapeDtypeStruct((tokens, listed), F32),
        ],
        scratch_shapes=[pltpu.VMEM((tokens, listed), F32)],
        compiler_params=VMEM,
        name="final_outputs",
    )(fetched, mix_a, mix_b, gate_a, cot, gate_b, slots_a)


def table_blocks(table):
    rows_dev, width = table.shape
    x1, x0 = lax.axis_index("x1"), lax.axis_index("x0")
    at_x, at_y, at_z = x1 * 2 + x0, lax.axis_index(RING), lax.axis_index("zh")
    n_y = lax.axis_size(RING)
    cut = table.reshape(rows_dev, 2, 4, 2, -1)
    cut = lax.dynamic_index_in_dim(cut, lax.axis_index(("zl0", "c")), 2, keepdims=False)
    cut = jnp.transpose(cut.reshape(rows_dev, 4, -1), (1, 0, 2))
    both = jnp.stack([cut, lax.ppermute(cut, "zh", [(0, 1), (1, 0)])], 1)
    mine = []
    for k in range(4):
        part = lax.dynamic_index_in_dim(both, at_x ^ k, 0, keepdims=False)
        if k:
            part = lax.ppermute(part, ("x1", "x0"), [(i, i ^ k) for i in range(4)])
        mine.append(part)
    block = jnp.stack(mine).reshape(4 * 2 * rows_dev, -1)
    ahead = [(i, (i + 1) % n_y) for i in range(n_y)]
    back = [(i, (i - 1) % n_y) for i in range(n_y)]
    blocks, origin = [block], [at_y]
    forward = backward = block
    for step in range(1, n_y // 2 + 1):
        forward = lax.ppermute(forward, RING, ahead)
        blocks.append(forward)
        origin.append((at_y - step) % n_y)
        if step < n_y - step:
            backward = lax.ppermute(backward, RING, back)
            blocks.append(backward)
            origin.append((at_y + step) % n_y)
    xs = at_x ^ jnp.arange(4, dtype=jnp.int32)
    zs = at_z ^ jnp.arange(2, dtype=jnp.int32)
    holder = (xs[None, :, None] * n_y + jnp.stack(origin)[:, None, None]) * 2 + zs[None, None, :]
    places = holder[..., None] * rows_dev + jnp.arange(rows_dev, dtype=jnp.int32)
    return blocks, places.reshape(len(blocks), -1).astype(F32)


def local(gate_a, cotangent_a, gate_b, table, row_ids, slots, weights):
    rows_dev = table.shape[0]
    owners = lax.axis_size(TABLE)
    listed = row_ids.shape[-1]
    gate_a, cotangent_a, gate_b = gate_a[0], cotangent_a[0], gate_b[0]
    lists = row_ids[0, :, 0]

    mix_a = mixing_of(slots[0, 0], weights[0, 0], listed)
    id_rows = jnp.stack([lists[0] // 64, lists[0] % 64, lists[1] // 64, lists[1] % 64]).astype(BF16)
    id_rows = jnp.concatenate([id_rows, jnp.zeros((12, listed), BF16)])
    sent = outgoing(gate_a, cotangent_a, mix_a, id_rows, 128)
    received = lax.all_to_all(sent, GRAD_GROUP, split_axis=0, concat_axis=0, tiled=True)

    blocks, places = table_blocks(table)

    codes = received[:, listed : listed + 4, :].astype(F32)
    ids = codes[:, 0::2] * 64.0 + codes[:, 1::2]
    dense = dense_rows(ids[:, 0], received, owners * rows_dev)
    arrived = lax.all_to_all(
        dense.reshape(owners, rows_dev, -1), TABLE, split_axis=0, concat_axis=0, tiled=True
    )

    near = ids.reshape(-1, 2, 2, listed)
    near = lax.dynamic_index_in_dim(near, lax.axis_index("y0"), 1, keepdims=False)
    picked = picked_rows(near, places, blocks)
    fetched = lax.all_to_all(picked, ROW_GROUP, split_axis=0, concat_axis=0, tiled=True)

    features = arrived.shape[-1]
    summed = jnp.sum(arrived.reshape(2, 2, -1, 2, 2, rows_dev, features).astype(F32), axis=(2, 4))
    mine = lax.axis_index("zl1")
    kept = lax.dynamic_index_in_dim(summed, mine, 0, keepdims=False)
    given = lax.dynamic_index_in_dim(summed, 1 - mine, 0, keepdims=False)
    total = kept + lax.ppermute(given, "zl1", [(0, 1), (1, 0)])
    grad_table = jnp.transpose(total, (2, 0, 1, 3)).reshape(rows_dev, -1)

    mix_b = mixing_of(slots[0, 1], weights[0, 1], listed)
    mixed_b, grad_gate, grad_weights = final_outputs(
        fetched, mix_a, mix_b, gate_a, cotangent_a, gate_b, slots[0, 0]
    )
    return mixed_b[None], grad_gate[None], grad_weights[None], grad_table


def solution(mesh):
    finer = Mesh(
        mesh.devices.reshape(2, 2, 2, 2, 2, 4, 2, 2),
        ("zl1", "zl0", "c", "x1", "x0", "y1", "y0", "zh"),
    )
    return jax.shard_map(
        local,
        mesh=finer,
        in_specs=(
            P(SECTION, TABLE, None),
            P(SECTION, TABLE, None),
            P(SECTION, TABLE, None),
            P(TABLE, None),
            P(SECTION, None, TABLE, None),
            P(SECTION, None, TABLE, None),
            P(SECTION, None, TABLE, None),
        ),
        out_specs=(
            P(SECTION, TABLE, None),
            P(SECTION, TABLE, None),
            P(SECTION, TABLE, None),
            P(TABLE, SECTION),
        ),
        check_vma=False,
    )
```

```python
import jax
import jax.numpy as jnp
from jax import lax
from jax.experimental import pallas as pl
from jax.experimental.pallas import tpu as pltpu
from jax.sharding import Mesh
from jax.sharding import PartitionSpec as P

SECTION = ("zl1", "zl0", "c")
TABLE = ("x1", "x0", "y1", "y0", "zh")
GRAD_GROUP = ("x1", "zl0", "c", "x0", "y0")
ROW_GROUP = ("x1", "zl0", "c", "x0")
RING = ("y1", "y0")
ROWS_DEV = 64
F32 = jnp.float32
BF16 = jnp.bfloat16
VMEM = pltpu.CompilerParams(vmem_limit_bytes=40 * 1024 * 1024)


def gated(gate, incoming):
    g = gate.astype(F32)
    sig = 1.0 / (1.0 + jnp.exp(-g))
    return g, sig, incoming.astype(F32)


def mixing_of(slots, weights):
    position = lax.broadcasted_iota(jnp.int32, slots.shape, 1)
    total = jnp.zeros(slots.shape, F32)
    for p in range(slots.shape[1]):
        total += jnp.where(slots[:, p : p + 1] == position, weights[:, p : p + 1], 0.0)
    return total.astype(BF16)


def outgoing_kernel(gate_ref, cot_ref, slots_ref, weights_ref, ids_ref, out_ref, mix_ref):
    listed = mix_ref.shape[1]

    @pl.when(pl.program_id(0) == 0)
    def _():
        mix_ref[...] = mixing_of(slots_ref[0, 0], weights_ref[0, 0])

    g, sig, inc = gated(gate_ref[0], cot_ref[0])
    grad_memory = (inc * g * sig).astype(BF16)
    rows = lax.dot_general(
        mix_ref[...], grad_memory, (((0,), (0,)), ((), ())), preferred_element_type=F32
    ).astype(BF16)
    ids = [ids_ref[0, c] for c in range(2)]
    codes = jnp.concatenate(
        [part for i in ids for part in (i // ROWS_DEV, i % ROWS_DEV)] + [jnp.zeros((12, listed), jnp.int32)]
    )
    codes = codes.astype(F32).astype(BF16)
    for k in range(out_ref.shape[0]):
        out_ref[k, :listed, :] = rows[:, k * 128 : (k + 1) * 128]
        out_ref[k, listed:, :] = codes


def outgoing(gate, cot, slots, weights, row_ids, features):
    _, tokens, width = gate.shape
    listed = row_ids.shape[-1]
    chunks, step = width // features, 8
    part = pl.BlockSpec((1, tokens, step * features), lambda i: (0, 0, i))
    picks = pl.BlockSpec((1, 1, tokens, listed), lambda i: (0, 0, 0, 0))
    return pl.pallas_call(
        outgoing_kernel,
        grid=(chunks // step,),
        in_specs=[part, part, picks, picks, pl.BlockSpec(row_ids.shape, lambda i: (0, 0, 0, 0))],
        out_specs=[
            pl.BlockSpec((step, listed + 16, features), lambda i: (i, 0, 0)),
            pl.BlockSpec((tokens, listed), lambda i: (0, 0)),
        ],
        out_shape=[
            jax.ShapeDtypeStruct((chunks, listed + 16, features), BF16),
            jax.ShapeDtypeStruct((tokens, listed), BF16),
        ],
        compiler_params=VMEM,
        name="outgoing_rows",
    )(gate, cot, slots, weights, row_ids)


def mixing_kernel(slots_ref, weights_ref, out_ref):
    out_ref[...] = mixing_of(slots_ref[0, 0], weights_ref[0, 0])


def mixing_b(slots, weights):
    tokens, listed = slots.shape[2:]
    picks = pl.BlockSpec((1, 1, tokens, listed), lambda i: (0, 1, 0, 0))
    return pl.pallas_call(
        mixing_kernel,
        grid=(1,),
        in_specs=[picks, picks],
        out_specs=pl.BlockSpec((tokens, listed), lambda i: (0, 0)),
        out_shape=jax.ShapeDtypeStruct((tokens, listed), BF16),
        compiler_params=VMEM,
        name="mixing_b",
    )(slots, weights)


def dense_kernel(ids_ref, rows_ref, out_ref):
    tile, features = out_ref.shape
    lists, listed = ids_ref.shape
    row = (lax.broadcasted_iota(jnp.int32, (tile, listed), 0) + pl.program_id(0) * tile).astype(F32)
    total = jnp.zeros((tile, features), F32)
    together = 8
    for first in range(0, lists, together):
        hot = [
            jnp.where(row == ids_ref[pl.ds(k, 1), :], 1.0, 0.0).astype(BF16)
            for k in range(first, first + together)
        ]
        rows = [rows_ref[k, :listed, :] for k in range(first, first + together)]
        total += jnp.dot(
            jnp.concatenate(hot, axis=1), jnp.concatenate(rows, axis=0), preferred_element_type=F32
        )
    out_ref[...] = total.astype(BF16)


def dense_rows(ids, received, rows):
    lists, listed = ids.shape
    features = received.shape[-1]
    tile = 256
    return pl.pallas_call(
        dense_kernel,
        grid=(rows // tile,),
        in_specs=[
            pl.BlockSpec((lists, listed), lambda i: (0, 0)),
            pl.BlockSpec(received.shape, lambda i: (0, 0, 0)),
        ],
        out_specs=pl.BlockSpec((tile, features), lambda i: (i, 0)),
        out_shape=jax.ShapeDtypeStruct((rows, features), BF16),
        compiler_params=VMEM,
        name="dense_rows",
    )(ids, received)


def pick_kernel(ids_ref, place_ref, *refs):
    blocks, out_ref = refs[:-1], refs[-1]
    lists, listed = ids_ref.shape[1:]
    wanted = jnp.concatenate(
        [jnp.transpose(jnp.broadcast_to(ids_ref[0, k : k + 1, :], (128, listed))) for k in range(lists)],
        axis=0,
    )
    total = jnp.zeros(out_ref.shape[1:], F32)
    for b, block in enumerate(blocks):
        rows = block.shape[0]
        hot = [
            jnp.where(wanted == place_ref[b : b + 1, q : q + 128], 1.0, 0.0).astype(BF16)
            for q in range(0, rows, 128)
        ]
        total += jnp.dot(jnp.concatenate(hot, axis=1), block[...], preferred_element_type=F32)
    out_ref[0] = total.astype(BF16)


def picked_rows(ids, places, blocks):
    members, lists, listed = ids.shape
    rows, features = blocks[0].shape
    return pl.pallas_call(
        pick_kernel,
        grid=(members,),
        in_specs=[
            pl.BlockSpec((1, lists, listed), lambda i: (i, 0, 0)),
            pl.BlockSpec(places.shape, lambda i: (0, 0)),
        ]
        + [pl.BlockSpec((rows, features), lambda i: (0, 0))] * len(blocks),
        out_specs=pl.BlockSpec((1, lists * listed, features), lambda i: (i, 0, 0)),
        out_shape=jax.ShapeDtypeStruct((members, lists * listed, features), BF16),
        compiler_params=VMEM,
        name="picked_rows",
    )(ids, places, *blocks)


def final_kernel(
    rows_ref, mix_a_ref, mix_b_ref, gate_a_ref, cot_ref, gate_b_ref, slots_ref,
    mixed_ref, grad_gate_ref, grad_weights_ref, scores_ref,
):
    listed = mix_a_ref.shape[1]
    step, _, features = rows_ref.shape

    @pl.when(pl.program_id(0) == 0)
    def _():
        scores_ref[...] = jnp.zeros_like(scores_ref)

    part = jnp.zeros(scores_ref.shape, F32)
    for k in range(step):
        at = slice(k * features, (k + 1) * features)
        fetched_a = rows_ref[k, :listed, :]
        fetched_b = rows_ref[k, listed:, :]
        memory_b = jnp.dot(mix_b_ref[...], fetched_b, preferred_element_type=F32)
        gb = gate_b_ref[0, :, at].astype(F32)
        mixed_ref[0, :, at] = (gb / (1.0 + jnp.exp(-gb)) * memory_b).astype(BF16)
        memory_a = jnp.dot(mix_a_ref[...], fetched_a, preferred_element_type=F32)
        g, sig, inc = gated(gate_a_ref[0, :, at], cot_ref[0, :, at])
        grad_gate_ref[0, :, at] = (inc * memory_a * sig * (1.0 + g * (1.0 - sig))).astype(BF16)
        grad_memory = (inc * g * sig).astype(BF16)
        part += lax.dot_general(
            grad_memory, fetched_a, (((1,), (1,)), ((), ())), preferred_element_type=F32
        )
    scores_ref[...] += part

    @pl.when(pl.program_id(0) == pl.num_programs(0) - 1)
    def _():
        grad_weights_ref[0] = jnp.take_along_axis(scores_ref[...], slots_ref[0, 0], axis=1)


def final_outputs(fetched, mix_a, mix_b, gate_a, cot, gate_b, slots):
    chunks, rows, features = fetched.shape
    _, tokens, width = gate_a.shape
    listed = mix_a.shape[1]
    step = 4
    whole = pl.BlockSpec((tokens, listed), lambda i: (0, 0))
    part = pl.BlockSpec((1, tokens, step * features), lambda i: (0, 0, i))
    return pl.pallas_call(
        final_kernel,
        grid=(chunks // step,),
        in_specs=[
            pl.BlockSpec((step, rows, features), lambda i: (i, 0, 0)),
            whole, whole, part, part, part,
            pl.BlockSpec((1, 1, tokens, listed), lambda i: (0, 0, 0, 0)),
        ],
        out_specs=[part, part, pl.BlockSpec((1, tokens, listed), lambda i: (0, 0, 0))],
        out_shape=[
            jax.ShapeDtypeStruct((1, tokens, width), BF16),
            jax.ShapeDtypeStruct((1, tokens, width), BF16),
            jax.ShapeDtypeStruct((1, tokens, listed), F32),
        ],
        scratch_shapes=[pltpu.VMEM((tokens, listed), F32)],
        compiler_params=VMEM,
        name="final_outputs",
    )(fetched, mix_a, mix_b, gate_a, cot, gate_b, slots)


def both_halves(table):
    rows_dev, width = table.shape
    cut = table.reshape(rows_dev, 2, 4, 2, -1)
    cut = lax.dynamic_index_in_dim(cut, lax.axis_index(("zl0", "c")), 2, keepdims=False)
    cut = jnp.transpose(cut.reshape(rows_dev, 4, -1), (1, 0, 2))
    return cut, lax.ppermute(cut, "zh", [(0, 1), (1, 0)])


def across_x(own, other):
    at_x = lax.axis_index(("x1", "x0"))
    mine = []
    for k in range(4):
        part = jnp.concatenate(
            [lax.dynamic_index_in_dim(h, at_x ^ k, 0, keepdims=False) for h in (own, other)]
        )
        if k:
            part = lax.ppermute(part, ("x1", "x0"), [(i, i ^ k) for i in range(4)])
        mine.append(part)
    return jnp.concatenate(mine)


def ring_step(forward, backward):
    n_y = lax.axis_size(RING)
    ahead = [(i, (i + 1) % n_y) for i in range(n_y)]
    back = [(i, (i - 1) % n_y) for i in range(n_y)]
    return (
        lax.ppermute(forward, RING, ahead),
        None if backward is None else lax.ppermute(backward, RING, back),
    )


def block_places(rows_dev, offsets):
    n_y = lax.axis_size(RING)
    xs = lax.axis_index(("x1", "x0")) ^ jnp.arange(4, dtype=jnp.int32)
    zs = lax.axis_index("zh") ^ jnp.arange(2, dtype=jnp.int32)
    ys = (lax.axis_index(RING) + jnp.array(offsets, jnp.int32)) & (n_y - 1)
    holder = (xs[None, :, None] * n_y + ys[:, None, None]) * 2 + zs[None, None, :]
    places = holder[..., None] * rows_dev + jnp.arange(rows_dev, dtype=jnp.int32)
    return places.reshape(len(offsets), -1).astype(F32)


def local(gate_a, cotangent_a, gate_b, table, row_ids, slots, weights):
    rows_dev = table.shape[0]
    owners = lax.axis_size(TABLE)
    listed = row_ids.shape[-1]

    own, other = both_halves(table)
    sent, mix_a = outgoing(gate_a, cotangent_a, slots, weights, row_ids, 128)
    sent, own, other = lax.optimization_barrier((sent, own, other))
    received = lax.all_to_all(sent, GRAD_GROUP, split_axis=0, concat_axis=0, tiled=True)
    block = across_x(own, other)
    received, block = lax.optimization_barrier((received, block))

    codes = received[:, listed : listed + 4, :].astype(F32)
    ids = codes[:, 0::2] * ROWS_DEV + codes[:, 1::2]
    dense = dense_rows(ids[:, 0], received, owners * rows_dev)
    f1, b1 = ring_step(block, block)
    dense, f1, b1 = lax.optimization_barrier((dense, f1, b1))
    arrived = lax.all_to_all(
        dense.reshape(owners, rows_dev, -1), TABLE, split_axis=0, concat_axis=0, tiled=True
    )
    f2, b2 = ring_step(f1, b1)
    f3, b3 = ring_step(f2, b2)
    f4, _ = ring_step(f3, None)

    near = ids.reshape(-1, 2, 2, listed)
    near = lax.dynamic_index_in_dim(near, lax.axis_index("y0"), 1, keepdims=False)
    places = block_places(rows_dev, (0, -1, 1, -2, 2, -3, 3, -4))
    picked = picked_rows(near, places, (block, f1, b1, f2, b2, f3, b3, f4))
    fetched = lax.all_to_all(picked, ROW_GROUP, split_axis=0, concat_axis=0, tiled=True)

    features = arrived.shape[-1]
    summed = jnp.sum(arrived.reshape(2, 2, -1, 2, 2, rows_dev, features).astype(F32), axis=(2, 4))
    mine = lax.axis_index("zl1")
    kept = lax.dynamic_index_in_dim(summed, mine, 0, keepdims=False)
    given = lax.dynamic_index_in_dim(summed, 1 - mine, 0, keepdims=False)
    total = kept + lax.ppermute(given, "zl1", [(0, 1), (1, 0)])
    grad_table = jnp.transpose(total, (2, 0, 1, 3)).reshape(rows_dev, -1)

    mix_b = mixing_b(slots, weights)
    mixed, grad_gate, grad_weights = final_outputs(
        fetched, mix_a, mix_b, gate_a, cotangent_a, gate_b, slots
    )
    return mixed, grad_gate, grad_weights, grad_table


def solution(mesh):
    finer = Mesh(
        mesh.devices.reshape(2, 2, 2, 2, 2, 4, 2, 2),
        ("zl1", "zl0", "c", "x1", "x0", "y1", "y0", "zh"),
    )
    return jax.shard_map(
        local,
        mesh=finer,
        in_specs=(
            P(SECTION, TABLE, None),
            P(SECTION, TABLE, None),
            P(SECTION, TABLE, None),
            P(TABLE, None),
            P(SECTION, None, TABLE, None),
            P(SECTION, None, TABLE, None),
            P(SECTION, None, TABLE, None),
        ),
        out_specs=(
            P(SECTION, TABLE, None),
            P(SECTION, TABLE, None),
            P(SECTION, TABLE, None),
            P(TABLE, SECTION),
        ),
        check_vma=False,
    )
```

```python
import jax
import jax.numpy as jnp
from jax import lax
from jax.experimental import pallas as pl
from jax.experimental.pallas import tpu as pltpu
from jax.sharding import Mesh
from jax.sharding import PartitionSpec as P

SECTION = ("zl1", "zl0", "c")
TABLE = ("x1", "x0", "y1", "y0", "zh")
GRAD_GROUP = ("x1", "zl0", "c", "x0", "y0")
ROW_GROUP = ("x1", "zl0", "c", "x0")
RING = ("y1", "y0")
ROWS_DEV = 64
F32 = jnp.float32
BF16 = jnp.bfloat16
VMEM = pltpu.CompilerParams(vmem_limit_bytes=40 * 1024 * 1024)
MOST_VMEM = pltpu.CompilerParams(vmem_limit_bytes=60 * 1024 * 1024)


def gated(gate, incoming):
    g = gate.astype(F32)
    sig = 1.0 / (1.0 + jnp.exp(-g))
    return g, sig, incoming.astype(F32)


def mixing_of(slots, weights):
    position = lax.broadcasted_iota(jnp.int32, slots.shape, 1)
    total = jnp.zeros(slots.shape, F32)
    for p in range(slots.shape[1]):
        total += jnp.where(slots[:, p : p + 1] == position, weights[:, p : p + 1], 0.0)
    return total.astype(BF16)


def outgoing_kernel(gate_ref, cot_ref, slots_ref, weights_ref, ids_ref, out_ref, mix_ref):
    listed = mix_ref.shape[1]

    @pl.when(pl.program_id(0) == 0)
    def _():
        mix_ref[...] = mixing_of(slots_ref[0, 0], weights_ref[0, 0])

    g, sig, inc = gated(gate_ref[0], cot_ref[0])
    grad_memory = (inc * g * sig).astype(BF16)
    rows = lax.dot_general(
        mix_ref[...], grad_memory, (((0,), (0,)), ((), ())), preferred_element_type=F32
    ).astype(BF16)
    ids = [ids_ref[0, c] for c in range(2)]
    codes = jnp.concatenate(
        [part for i in ids for part in (i // ROWS_DEV, i % ROWS_DEV)] + [jnp.zeros((12, listed), jnp.int32)]
    )
    codes = codes.astype(F32).astype(BF16)
    for k in range(out_ref.shape[0]):
        out_ref[k, :listed, :] = rows[:, k * 128 : (k + 1) * 128]
        out_ref[k, listed:, :] = codes


def outgoing(gate, cot, slots, weights, row_ids, features):
    _, tokens, width = gate.shape
    listed = row_ids.shape[-1]
    chunks, step = width // features, 8
    part = pl.BlockSpec((1, tokens, step * features), lambda i: (0, 0, i))
    picks = pl.BlockSpec((1, 1, tokens, listed), lambda i: (0, 0, 0, 0))
    return pl.pallas_call(
        outgoing_kernel,
        grid=(chunks // step,),
        in_specs=[part, part, picks, picks, pl.BlockSpec(row_ids.shape, lambda i: (0, 0, 0, 0))],
        out_specs=[
            pl.BlockSpec((step, listed + 16, features), lambda i: (i, 0, 0)),
            pl.BlockSpec((tokens, listed), lambda i: (0, 0)),
        ],
        out_shape=[
            jax.ShapeDtypeStruct((chunks, listed + 16, features), BF16),
            jax.ShapeDtypeStruct((tokens, listed), BF16),
        ],
        compiler_params=MOST_VMEM,
        name="outgoing_rows",
    )(gate, cot, slots, weights, row_ids)


def factors_kernel(
    gate_a_ref, cot_ref, gate_b_ref, slots_ref, weights_ref,
    to_gate_ref, to_memory_ref, swish_ref, mix_ref,
):
    @pl.when(pl.program_id(0) == 0)
    def _():
        mix_ref[...] = mixing_of(slots_ref[0, 0], weights_ref[0, 0])

    g, sig, inc = gated(gate_a_ref[0], cot_ref[0])
    to_gate_ref[...] = inc * sig * (1.0 + g * (1.0 - sig))
    to_memory_ref[...] = (inc * g * sig).astype(BF16)
    gb = gate_b_ref[0].astype(F32)
    swish_ref[...] = gb / (1.0 + jnp.exp(-gb))


def factors(gate_a, cot, gate_b, slots, weights):
    _, tokens, width = gate_a.shape
    listed = slots.shape[-1]
    cols = width // 2
    part = pl.BlockSpec((1, tokens, cols), lambda i: (0, 0, i))
    out = pl.BlockSpec((tokens, cols), lambda i: (0, i))
    picks = pl.BlockSpec((1, 1, tokens, listed), lambda i: (0, 1, 0, 0))
    return pl.pallas_call(
        factors_kernel,
        grid=(width // cols,),
        in_specs=[part, part, part, picks, picks],
        out_specs=[out, out, out, pl.BlockSpec((tokens, listed), lambda i: (0, 0))],
        out_shape=[
            jax.ShapeDtypeStruct((tokens, width), F32),
            jax.ShapeDtypeStruct((tokens, width), BF16),
            jax.ShapeDtypeStruct((tokens, width), F32),
            jax.ShapeDtypeStruct((tokens, listed), BF16),
        ],
        compiler_params=MOST_VMEM,
        name="factors",
    )(gate_a, cot, gate_b, slots, weights)


def dense_kernel(ids_ref, rows_ref, out_ref):
    tile, features = out_ref.shape
    lists, listed = ids_ref.shape
    row = (lax.broadcasted_iota(jnp.int32, (tile, listed), 0) + pl.program_id(0) * tile).astype(F32)
    total = jnp.zeros((tile, features), F32)
    together = 8
    for first in range(0, lists, together):
        hot = [
            jnp.where(row == ids_ref[pl.ds(k, 1), :], 1.0, 0.0).astype(BF16)
            for k in range(first, first + together)
        ]
        rows = [rows_ref[k, :listed, :] for k in range(first, first + together)]
        total += jnp.dot(
            jnp.concatenate(hot, axis=1), jnp.concatenate(rows, axis=0), preferred_element_type=F32
        )
    out_ref[...] = total.astype(BF16)


def dense_rows(ids, received, rows):
    lists, listed = ids.shape
    features = received.shape[-1]
    tile = 256
    return pl.pallas_call(
        dense_kernel,
        grid=(rows // tile,),
        in_specs=[
            pl.BlockSpec((lists, listed), lambda i: (0, 0)),
            pl.BlockSpec(received.shape, lambda i: (0, 0, 0)),
        ],
        out_specs=pl.BlockSpec((tile, features), lambda i: (i, 0)),
        out_shape=jax.ShapeDtypeStruct((rows, features), BF16),
        compiler_params=VMEM,
        name="dense_rows",
    )(ids, received)


def pick_kernel(ids_ref, place_ref, *refs):
    blocks, out_ref = refs[:-1], refs[-1]
    lists, listed = ids_ref.shape[1:]
    wanted = jnp.concatenate(
        [jnp.transpose(jnp.broadcast_to(ids_ref[0, k : k + 1, :], (128, listed))) for k in range(lists)],
        axis=0,
    )
    total = jnp.zeros(out_ref.shape[1:], F32)
    for b, block in enumerate(blocks):
        rows = block.shape[0]
        hot = [
            jnp.where(wanted == place_ref[b : b + 1, q : q + 128], 1.0, 0.0).astype(BF16)
            for q in range(0, rows, 128)
        ]
        total += jnp.dot(jnp.concatenate(hot, axis=1), block[...], preferred_element_type=F32)
    out_ref[0] = total.astype(BF16)


def picked_rows(ids, places, blocks):
    members, lists, listed = ids.shape
    rows, features = blocks[0].shape
    return pl.pallas_call(
        pick_kernel,
        grid=(members,),
        in_specs=[
            pl.BlockSpec((1, lists, listed), lambda i: (i, 0, 0)),
            pl.BlockSpec(places.shape, lambda i: (0, 0)),
        ]
        + [pl.BlockSpec((rows, features), lambda i: (0, 0))] * len(blocks),
        out_specs=pl.BlockSpec((1, lists * listed, features), lambda i: (i, 0, 0)),
        out_shape=jax.ShapeDtypeStruct((members, lists * listed, features), BF16),
        compiler_params=MOST_VMEM,
        name="picked_rows",
    )(ids, places, *blocks)


def final_kernel(
    rows_ref, mix_a_ref, mix_b_ref, to_gate_ref, to_memory_ref, swish_ref, slots_ref,
    mixed_ref, grad_gate_ref, grad_weights_ref, scores_ref,
):
    listed = mix_a_ref.shape[1]
    step, _, features = rows_ref.shape

    @pl.when(pl.program_id(0) == 0)
    def _():
        scores_ref[...] = jnp.zeros_like(scores_ref)

    part = jnp.zeros(scores_ref.shape, F32)
    for k in range(step):
        at = slice(k * features, (k + 1) * features)
        fetched_a = rows_ref[k, :listed, :]
        fetched_b = rows_ref[k, listed:, :]
        memory_b = jnp.dot(mix_b_ref[...], fetched_b, preferred_element_type=F32)
        mixed_ref[0, :, at] = (swish_ref[:, at] * memory_b).astype(BF16)
        memory_a = jnp.dot(mix_a_ref[...], fetched_a, preferred_element_type=F32)
        grad_gate_ref[0, :, at] = (to_gate_ref[:, at] * memory_a).astype(BF16)
        part += lax.dot_general(
            to_memory_ref[:, at], fetched_a, (((1,), (1,)), ((), ())), preferred_element_type=F32
        )
    scores_ref[...] += part

    @pl.when(pl.program_id(0) == pl.num_programs(0) - 1)
    def _():
        grad_weights_ref[0] = jnp.take_along_axis(scores_ref[...], slots_ref[0, 0], axis=1)


def final_outputs(fetched, mix_a, mix_b, to_gate, to_memory, swish, slots):
    chunks, rows, features = fetched.shape
    tokens, width = to_gate.shape
    listed = mix_a.shape[1]
    step = 4
    whole = pl.BlockSpec((tokens, listed), lambda i: (0, 0))
    part = pl.BlockSpec((tokens, step * features), lambda i: (0, i))
    out = pl.BlockSpec((1, tokens, step * features), lambda i: (0, 0, i))
    return pl.pallas_call(
        final_kernel,
        grid=(chunks // step,),
        in_specs=[
            pl.BlockSpec((step, rows, features), lambda i: (i, 0, 0)),
            whole, whole, part, part, part,
            pl.BlockSpec((1, 1, tokens, listed), lambda i: (0, 0, 0, 0)),
        ],
        out_specs=[out, out, pl.BlockSpec((1, tokens, listed), lambda i: (0, 0, 0))],
        out_shape=[
            jax.ShapeDtypeStruct((1, tokens, width), BF16),
            jax.ShapeDtypeStruct((1, tokens, width), BF16),
            jax.ShapeDtypeStruct((1, tokens, listed), F32),
        ],
        scratch_shapes=[pltpu.VMEM((tokens, listed), F32)],
        compiler_params=MOST_VMEM,
        name="final_outputs",
    )(fetched, mix_a, mix_b, to_gate, to_memory, swish, slots)


def features_for(table, zl0):
    rows_dev, width = table.shape
    at = (zl0 * 2 + lax.axis_index("c")) * (width // 8)
    return jnp.stack(
        [lax.dynamic_slice(table, (0, at + h * (width // 2)), (rows_dev, width // 8)) for h in range(2)]
    )


def both_halves(table):
    zl0 = lax.axis_index("zl0")
    mirrored = lax.ppermute(features_for(table, 1 - zl0), ("zl1", "zl0", "zh"), [(i, 7 - i) for i in range(8)])
    return features_for(table, zl0), mirrored


def across_x(own, other):
    at_x = lax.axis_index(("x1", "x0"))
    rows, half = own.shape[1], own.shape[2] // 2
    mine = []
    for k in range(4):
        to = at_x ^ k
        part = jnp.concatenate(
            [
                lax.dynamic_slice(h, (to // 2, 0, (to % 2) * half), (1, rows, half))[0]
                for h in (own, other)
            ]
        )
        if k:
            part = lax.ppermute(part, ("x1", "x0"), [(i, i ^ k) for i in range(4)])
        mine.append(part)
    return jnp.concatenate(mine)


def ring_step(forward, backward):
    n_y = lax.axis_size(RING)
    ahead = [(i, (i + 1) % n_y) for i in range(n_y)]
    back = [(i, (i - 1) % n_y) for i in range(n_y)]
    return (
        lax.ppermute(forward, RING, ahead),
        None if backward is None else lax.ppermute(backward, RING, back),
    )


def block_places(rows_dev, offsets):
    n_y = lax.axis_size(RING)
    xs = lax.axis_index(("x1", "x0")) ^ jnp.arange(4, dtype=jnp.int32)
    zs = lax.axis_index("zh") ^ jnp.arange(2, dtype=jnp.int32)
    ys = (lax.axis_index(RING) + jnp.array(offsets, jnp.int32)) & (n_y - 1)
    holder = (xs[None, :, None] * n_y + ys[:, None, None]) * 2 + zs[None, None, :]
    places = holder[..., None] * rows_dev + jnp.arange(rows_dev, dtype=jnp.int32)
    return places.reshape(len(offsets), -1).astype(F32)


def local(gate_a, cotangent_a, gate_b, table, row_ids, slots, weights):
    rows_dev = table.shape[0]
    owners = lax.axis_size(TABLE)
    listed = row_ids.shape[-1]

    own, other = both_halves(table)
    sent, mix_a = outgoing(gate_a, cotangent_a, slots, weights, row_ids, 128)
    sent, other = lax.optimization_barrier((sent, other))
    block = across_x(own, other)
    sent, block = lax.optimization_barrier((sent, block))
    received = lax.all_to_all(sent, GRAD_GROUP, split_axis=0, concat_axis=0, tiled=True)
    f1, b1 = ring_step(block, block)
    f2, b2 = ring_step(f1, b1)
    received, f2, b2 = lax.optimization_barrier((received, f2, b2))

    codes = received[:, listed : listed + 4, :].astype(F32)
    ids = codes[:, 0::2] * ROWS_DEV + codes[:, 1::2]
    dense = dense_rows(ids[:, 0], received, owners * rows_dev)
    f3, b3 = ring_step(f2, b2)
    dense, f3, b3 = lax.optimization_barrier((dense, f3, b3))
    arrived = lax.all_to_all(
        dense.reshape(owners, rows_dev, -1), TABLE, split_axis=0, concat_axis=0, tiled=True
    )
    f4, _ = ring_step(f3, None)

    near = ids.reshape(-1, 2, 2, listed)
    near = lax.dynamic_index_in_dim(near, lax.axis_index("y0"), 1, keepdims=False)
    places = block_places(rows_dev, (0, -1, 1, -2, 2, -3, 3, -4))
    picked = picked_rows(near, places, (block, f1, b1, f2, b2, f3, b3, f4))
    fetched = lax.all_to_all(picked, ROW_GROUP, split_axis=0, concat_axis=0, tiled=True)

    features = arrived.shape[-1]
    summed = jnp.sum(arrived.reshape(2, 2, -1, 2, 2, rows_dev, features).astype(F32), axis=(2, 4))
    mine = lax.axis_index("zl1")
    kept = lax.dynamic_index_in_dim(summed, mine, 0, keepdims=False)
    given = lax.dynamic_index_in_dim(summed, 1 - mine, 0, keepdims=False)
    total = kept + lax.ppermute(given, "zl1", [(0, 1), (1, 0)])
    grad_table = jnp.transpose(total, (2, 0, 1, 3)).reshape(rows_dev, -1)

    picked_first = lax.optimization_barrier((picked, gate_a, cotangent_a, gate_b))
    to_gate, to_memory, swish, mix_b = factors(*picked_first[1:], slots, weights)
    mixed, grad_gate, grad_weights = final_outputs(
        fetched, mix_a, mix_b, to_gate, to_memory, swish, slots
    )
    return mixed, grad_gate, grad_weights, grad_table


def solution(mesh):
    finer = Mesh(
        mesh.devices.reshape(2, 2, 2, 2, 2, 4, 2, 2),
        ("zl1", "zl0", "c", "x1", "x0", "y1", "y0", "zh"),
    )
    return jax.shard_map(
        local,
        mesh=finer,
        in_specs=(
            P(SECTION, TABLE, None),
            P(SECTION, TABLE, None),
            P(SECTION, TABLE, None),
            P(TABLE, None),
            P(SECTION, None, TABLE, None),
            P(SECTION, None, TABLE, None),
            P(SECTION, None, TABLE, None),
        ),
        out_specs=(
            P(SECTION, TABLE, None),
            P(SECTION, TABLE, None),
            P(SECTION, TABLE, None),
            P(TABLE, SECTION),
        ),
        check_vma=False,
    )
```

```python
import jax
import jax.numpy as jnp
from jax import lax
from jax.experimental import pallas as pl
from jax.experimental.pallas import tpu as pltpu
from jax.sharding import Mesh
from jax.sharding import PartitionSpec as P

SECTION = ("zl1", "zl0", "c")
TABLE = ("x1", "x0", "y1", "y0", "zh")
GRAD_GROUP = ("x1", "zl0", "c", "x0", "y0")
ROW_GROUP = ("x1", "zl0", "c", "x0")
RING = ("y1", "y0")
ROWS_DEV = 64
F32 = jnp.float32
BF16 = jnp.bfloat16
VMEM = pltpu.CompilerParams(vmem_limit_bytes=40 * 1024 * 1024)
MOST_VMEM = pltpu.CompilerParams(vmem_limit_bytes=60 * 1024 * 1024)


def gated(gate, incoming):
    g = gate.astype(F32)
    sig = 1.0 / (1.0 + jnp.exp(-g))
    return g, sig, incoming.astype(F32)


def mixing_of(slots, weights):
    position = lax.broadcasted_iota(jnp.int32, slots.shape, 1)
    total = jnp.zeros(slots.shape, F32)
    for p in range(slots.shape[1]):
        total += jnp.where(slots[:, p : p + 1] == position, weights[:, p : p + 1], 0.0)
    return total.astype(BF16)


def mixing_kernel(slots_ref, weights_ref, out_ref):
    out_ref[0] = mixing_of(slots_ref[0, 0], weights_ref[0, 0])


def mixing(slots, weights):
    tokens, listed = slots.shape[2:]
    picks = pl.BlockSpec((1, 1, tokens, listed), lambda c: (0, c, 0, 0))
    return pl.pallas_call(
        mixing_kernel,
        grid=(2,),
        in_specs=[picks, picks],
        out_specs=pl.BlockSpec((1, tokens, listed), lambda c: (c, 0, 0)),
        out_shape=jax.ShapeDtypeStruct((2, tokens, listed), BF16),
        compiler_params=MOST_VMEM,
        name="mixing",
    )(slots, weights)


def outgoing_kernel(gate_ref, cot_ref, mix_ref, ids_ref, own_ref, other_ref, out_ref):
    listed = mix_ref.shape[2]
    g, sig, inc = gated(gate_ref[0], cot_ref[0])
    grad_memory = (inc * g * sig).astype(BF16)
    rows = lax.dot_general(
        mix_ref[0], grad_memory, (((0,), (0,)), ((), ())), preferred_element_type=F32
    ).astype(BF16)
    ids = [ids_ref[0, c] for c in range(2)]
    codes = jnp.concatenate(
        [part for i in ids for part in (i // ROWS_DEV, i % ROWS_DEV)] + [jnp.zeros((12, listed), jnp.int32)]
    )
    codes = codes.astype(F32).astype(BF16)
    table = jnp.concatenate([own_ref[...], other_ref[...]])
    held = table.shape[0]
    for k in range(out_ref.shape[0]):
        at = (k // 2) * 256
        out_ref[k, :listed, :] = rows[:, k * 128 : (k + 1) * 128]
        out_ref[k, listed : listed + 16, :] = codes
        out_ref[k, listed + 16 : listed + 16 + held, :] = table[:, at : at + 128]
        out_ref[k, listed + 16 + held :, :] = table[:, at + 128 : at + 256]


def outgoing(gate, cot, mix, row_ids, own, other, features):
    _, tokens, width = gate.shape
    listed, held = row_ids.shape[-1], own.shape[0]
    chunks, step = width // features, 8
    part = pl.BlockSpec((1, tokens, step * features), lambda i: (0, 0, i))
    rows = pl.BlockSpec((held, step * features), lambda i: (0, i))
    height = listed + 16 + 4 * held
    return pl.pallas_call(
        outgoing_kernel,
        grid=(chunks // step,),
        in_specs=[
            part, part,
            pl.BlockSpec((1, tokens, listed), lambda i: (0, 0, 0)),
            pl.BlockSpec(row_ids.shape, lambda i: (0, 0, 0, 0)),
            rows, rows,
        ],
        out_specs=pl.BlockSpec((step, height, features), lambda i: (i, 0, 0)),
        out_shape=jax.ShapeDtypeStruct((chunks, height, features), BF16),
        compiler_params=MOST_VMEM,
        name="outgoing_rows",
    )(gate, cot, mix, row_ids, own, other)


def dense_kernel(ids_ref, rows_ref, out_ref):
    tile, features = out_ref.shape
    lists, listed = ids_ref.shape
    row = (lax.broadcasted_iota(jnp.int32, (tile, listed), 0) + pl.program_id(0) * tile).astype(F32)
    total = jnp.zeros((tile, features), F32)
    together = 8
    for first in range(0, lists, together):
        hot = [
            jnp.where(row == ids_ref[pl.ds(k, 1), :], 1.0, 0.0).astype(BF16)
            for k in range(first, first + together)
        ]
        rows = [rows_ref[k, :listed, :] for k in range(first, first + together)]
        total += jnp.dot(
            jnp.concatenate(hot, axis=1), jnp.concatenate(rows, axis=0), preferred_element_type=F32
        )
    out_ref[...] = total.astype(BF16)


def dense_rows(ids, received, rows):
    lists, listed = ids.shape
    features = received.shape[-1]
    tile = 256
    return pl.pallas_call(
        dense_kernel,
        grid=(rows // tile,),
        in_specs=[
            pl.BlockSpec((lists, listed), lambda i: (0, 0)),
            pl.BlockSpec(received.shape, lambda i: (0, 0, 0)),
        ],
        out_specs=pl.BlockSpec((tile, features), lambda i: (i, 0)),
        out_shape=jax.ShapeDtypeStruct((rows, features), BF16),
        compiler_params=VMEM,
        name="dense_rows",
    )(ids, received)


def pick_kernel(ids_ref, place_ref, *refs):
    blocks, out_ref = refs[:-1], refs[-1]
    lists, listed = ids_ref.shape[1:]
    wanted = jnp.concatenate(
        [jnp.transpose(jnp.broadcast_to(ids_ref[0, k : k + 1, :], (128, listed))) for k in range(lists)],
        axis=0,
    )
    total = jnp.zeros(out_ref.shape[1:], F32)
    for b, block in enumerate(blocks):
        rows = block.shape[0]
        hot = [
            jnp.where(wanted == place_ref[b : b + 1, q : q + 128], 1.0, 0.0).astype(BF16)
            for q in range(0, rows, 128)
        ]
        total += jnp.dot(jnp.concatenate(hot, axis=1), block[...], preferred_element_type=F32)
    out_ref[0] = total.astype(BF16)


def picked_rows(ids, places, blocks):
    members, lists, listed = ids.shape
    rows, features = blocks[0].shape
    return pl.pallas_call(
        pick_kernel,
        grid=(members,),
        in_specs=[
            pl.BlockSpec((1, lists, listed), lambda i: (i, 0, 0)),
            pl.BlockSpec(places.shape, lambda i: (0, 0)),
        ]
        + [pl.BlockSpec((rows, features), lambda i: (0, 0))] * len(blocks),
        out_specs=pl.BlockSpec((1, lists * listed, features), lambda i: (i, 0, 0)),
        out_shape=jax.ShapeDtypeStruct((members, lists * listed, features), BF16),
        compiler_params=VMEM,
        name="picked_rows",
    )(ids, places, *blocks)


def final_kernel(
    rows_ref, mix_a_ref, mix_b_ref, gate_a_ref, cot_ref, gate_b_ref, slots_ref,
    mixed_ref, grad_gate_ref, grad_weights_ref, scores_ref,
):
    listed = mix_a_ref.shape[2]
    step, _, features = rows_ref.shape

    @pl.when(pl.program_id(0) == 0)
    def _():
        scores_ref[...] = jnp.zeros_like(scores_ref)

    part = jnp.zeros(scores_ref.shape, F32)
    for k in range(step):
        at = slice(k * features, (k + 1) * features)
        fetched_a = rows_ref[k, :listed, :]
        fetched_b = rows_ref[k, listed:, :]
        memory_b = jnp.dot(mix_b_ref[0], fetched_b, preferred_element_type=F32)
        gb = gate_b_ref[0, :, at].astype(F32)
        mixed_ref[0, :, at] = (gb / (1.0 + jnp.exp(-gb)) * memory_b).astype(BF16)
        memory_a = jnp.dot(mix_a_ref[0], fetched_a, preferred_element_type=F32)
        g, sig, inc = gated(gate_a_ref[0, :, at], cot_ref[0, :, at])
        grad_gate_ref[0, :, at] = (inc * memory_a * sig * (1.0 + g * (1.0 - sig))).astype(BF16)
        grad_memory = (inc * g * sig).astype(BF16)
        part += lax.dot_general(
            grad_memory, fetched_a, (((1,), (1,)), ((), ())), preferred_element_type=F32
        )
    scores_ref[...] += part

    @pl.when(pl.program_id(0) == pl.num_programs(0) - 1)
    def _():
        grad_weights_ref[0] = jnp.take_along_axis(scores_ref[...], slots_ref[0, 0], axis=1)


def final_outputs(fetched, mix, gate_a, cot, gate_b, slots):
    chunks, rows, features = fetched.shape
    _, tokens, width = gate_a.shape
    listed = mix.shape[-1]
    step = 4
    part = pl.BlockSpec((1, tokens, step * features), lambda i: (0, 0, i))
    return pl.pallas_call(
        final_kernel,
        grid=(chunks // step,),
        in_specs=[
            pl.BlockSpec((step, rows, features), lambda i: (i, 0, 0)),
            pl.BlockSpec((1, tokens, listed), lambda i: (0, 0, 0)),
            pl.BlockSpec((1, tokens, listed), lambda i: (1, 0, 0)),
            part, part, part,
            pl.BlockSpec((1, 1, tokens, listed), lambda i: (0, 0, 0, 0)),
        ],
        out_specs=[part, part, pl.BlockSpec((1, tokens, listed), lambda i: (0, 0, 0))],
        out_shape=[
            jax.ShapeDtypeStruct((1, tokens, width), BF16),
            jax.ShapeDtypeStruct((1, tokens, width), BF16),
            jax.ShapeDtypeStruct((1, tokens, listed), F32),
        ],
        scratch_shapes=[pltpu.VMEM((tokens, listed), F32)],
        compiler_params=VMEM,
        name="final_outputs",
    )(fetched, mix, mix, gate_a, cot, gate_b, slots)


def quarters(table):
    rows = table.shape[0] // 4
    zl0, core = lax.axis_index("zl0"), lax.axis_index("c")

    def quarter(z):
        return lax.dynamic_slice_in_dim(table, (z * 2 + core) * rows, rows, 0)

    mirrored = [(i, 7 - i) for i in range(8)]
    return quarter(zl0), lax.ppermute(quarter(1 - zl0), ("zl1", "zl0", "zh"), mirrored)


def along_y(block, inner):
    n_y = lax.axis_size(RING)
    if inner:
        pairs = [(i, i ^ 1) for i in range(n_y)]
    else:
        pairs = [(i, (i + 1) % n_y if i % 2 else (i - 1) % n_y) for i in range(n_y)]
    return lax.ppermute(block, RING, pairs)


def block_places(members, held):
    n_x, n_pairs = 4, lax.axis_size("y1")
    y0, pair = lax.axis_index("y0"), lax.axis_index("y1")
    turn = 2 * y0 - 1
    pairs = (pair + jnp.stack([jnp.zeros_like(turn), turn, -turn, 2 * jnp.ones_like(turn)])) & (n_pairs - 1)
    member = jnp.arange(members, dtype=jnp.int32)
    x = (member >> 4) * 2 + ((member >> 1) & 1)
    quarter, y_low = (member >> 2) & 3, member & 1
    zh = lax.axis_index("zh") ^ jnp.arange(2, dtype=jnp.int32)
    y = pairs[:, None] * 2 + y_low[None, :]
    holder = (x[None, :, None] * (2 * n_pairs) + y[:, :, None]) * 2 + zh[None, None, :]
    row = holder * ROWS_DEV + (quarter * held)[None, :, None]
    places = row[..., None] + jnp.arange(held, dtype=jnp.int32)
    return places.reshape(n_pairs, -1).astype(F32)


def local(gate_a, cotangent_a, gate_b, table, row_ids, slots, weights):
    rows_dev = table.shape[0]
    owners = lax.axis_size(TABLE)
    listed = row_ids.shape[-1]

    own, other = quarters(table)
    mix = mixing(slots, weights)
    mix, other = lax.optimization_barrier((mix, other))
    sent = outgoing(gate_a, cotangent_a, mix, row_ids, own, other, 128)
    received = lax.all_to_all(sent, GRAD_GROUP, split_axis=0, concat_axis=0, tiled=True)

    members, held = received.shape[0], own.shape[0]
    first = listed + 16
    halves = [
        received[:, at : at + 2 * held].reshape(members * 2 * held, -1) for at in (first, first + 2 * held)
    ]
    block = jnp.concatenate(halves, axis=1)
    codes = received[:, listed : listed + 4, :].astype(F32)
    ids = codes[:, 0::2] * ROWS_DEV + codes[:, 1::2]
    dense = dense_rows(ids[:, 0], received, owners * rows_dev)
    next_1 = along_y(block, False)
    dense, next_1 = lax.optimization_barrier((dense, next_1))
    arrived = lax.all_to_all(
        dense.reshape(owners, rows_dev, -1), TABLE, split_axis=0, concat_axis=0, tiled=True
    )
    next_2 = along_y(next_1, True)
    next_3 = along_y(next_2, False)

    near = ids.reshape(-1, 2, 2, listed)
    near = lax.dynamic_index_in_dim(near, lax.axis_index("y0"), 1, keepdims=False)
    picked = picked_rows(near, block_places(members, held), (block, next_1, next_2, next_3))
    fetched = lax.all_to_all(picked, ROW_GROUP, split_axis=0, concat_axis=0, tiled=True)

    features = arrived.shape[-1]
    summed = jnp.sum(arrived.reshape(2, 2, -1, 2, 2, rows_dev, features).astype(F32), axis=(2, 4))
    mine = lax.axis_index("zl1")
    kept = lax.dynamic_index_in_dim(summed, mine, 0, keepdims=False)
    given = lax.dynamic_index_in_dim(summed, 1 - mine, 0, keepdims=False)
    total = kept + lax.ppermute(given, "zl1", [(0, 1), (1, 0)])
    grad_table = jnp.transpose(total, (2, 0, 1, 3)).reshape(rows_dev, -1)

    mixed, grad_gate, grad_weights = final_outputs(fetched, mix, gate_a, cotangent_a, gate_b, slots)
    return mixed, grad_gate, grad_weights, grad_table


def solution(mesh):
    finer = Mesh(
        mesh.devices.reshape(2, 2, 2, 2, 2, 4, 2, 2),
        ("zl1", "zl0", "c", "x1", "x0", "y1", "y0", "zh"),
    )
    return jax.shard_map(
        local,
        mesh=finer,
        in_specs=(
            P(SECTION, TABLE, None),
            P(SECTION, TABLE, None),
            P(SECTION, TABLE, None),
            P(TABLE, None),
            P(SECTION, None, TABLE, None),
            P(SECTION, None, TABLE, None),
            P(SECTION, None, TABLE, None),
        ),
        out_specs=(
            P(SECTION, TABLE, None),
            P(SECTION, TABLE, None),
            P(SECTION, TABLE, None),
            P(TABLE, SECTION),
        ),
        check_vma=False,
    )
```

```python
import jax
import jax.numpy as jnp
from jax import lax
from jax.experimental import pallas as pl
from jax.experimental.pallas import tpu as pltpu
from jax.sharding import Mesh
from jax.sharding import PartitionSpec as P

SECTION = ("zl1", "zl0", "c")
TABLE = ("x1", "x0", "y1", "y0", "zh")
GROUP = ("x1", "zl0", "c", "x0", "y0")
RING = ("y1", "y0")
ROWS_DEV = 64
AWAY = (-1, 1, 2)
F32 = jnp.float32
BF16 = jnp.bfloat16
VMEM = pltpu.CompilerParams(vmem_limit_bytes=40 * 1024 * 1024)
MOST_VMEM = pltpu.CompilerParams(vmem_limit_bytes=60 * 1024 * 1024)


def gated(gate, incoming):
    g = gate.astype(F32)
    sig = 1.0 / (1.0 + jnp.exp(-g))
    return g, sig, incoming.astype(F32)


def mixing_of(slots, weights):
    position = lax.broadcasted_iota(jnp.int32, slots.shape, 1)
    total = jnp.zeros(slots.shape, F32)
    for p in range(slots.shape[1]):
        total += jnp.where(slots[:, p : p + 1] == position, weights[:, p : p + 1], 0.0)
    return total.astype(BF16)


def mixing_kernel(slots_ref, weights_ref, out_ref):
    out_ref[...] = mixing_of(slots_ref[0, 0], weights_ref[0, 0])


def mixing(slots, weights, batch):
    tokens, listed = slots.shape[2:]
    picks = pl.BlockSpec((1, 1, tokens, listed), lambda i: (0, batch, 0, 0))
    return pl.pallas_call(
        mixing_kernel,
        grid=(1,),
        in_specs=[picks, picks],
        out_specs=pl.BlockSpec((tokens, listed), lambda i: (0, 0)),
        out_shape=jax.ShapeDtypeStruct((tokens, listed), BF16),
        compiler_params=MOST_VMEM,
        name="mixing",
    )(slots, weights)


def outgoing_kernel(gate_ref, cot_ref, mix_ref, ids_ref, own_ref, other_ref, out_ref):
    listed = mix_ref.shape[1]
    g, sig, inc = gated(gate_ref[0], cot_ref[0])
    grad_memory = (inc * g * sig).astype(BF16)
    rows = lax.dot_general(
        mix_ref[...], grad_memory, (((0,), (0,)), ((), ())), preferred_element_type=F32
    ).astype(BF16)
    ids = [ids_ref[0, c] for c in range(2)]
    codes = jnp.concatenate(
        [part for i in ids for part in (i // ROWS_DEV, i % ROWS_DEV)] + [jnp.zeros((12, listed), jnp.int32)]
    )
    codes = codes.astype(F32).astype(BF16)
    table = jnp.concatenate([own_ref[...], other_ref[...]])
    for k in range(out_ref.shape[0]):
        at = slice(k * 128, (k + 1) * 128)
        out_ref[k, :listed, :] = rows[:, at]
        out_ref[k, listed : listed + 16, :] = codes
        out_ref[k, listed + 16 :, :] = table[:, at]


def outgoing(gate, cot, mix, row_ids, own, other, features):
    _, tokens, width = gate.shape
    listed, held = row_ids.shape[-1], own.shape[0]
    chunks, step = width // features, 8
    part = pl.BlockSpec((1, tokens, step * features), lambda i: (0, 0, i))
    rows = pl.BlockSpec((held, step * features), lambda i: (0, i))
    height = listed + 16 + 2 * held
    return pl.pallas_call(
        outgoing_kernel,
        grid=(chunks // step,),
        in_specs=[
            part, part,
            pl.BlockSpec((tokens, listed), lambda i: (0, 0)),
            pl.BlockSpec(row_ids.shape, lambda i: (0, 0, 0, 0)),
            rows, rows,
        ],
        out_specs=pl.BlockSpec((step, height, features), lambda i: (i, 0, 0)),
        out_shape=jax.ShapeDtypeStruct((chunks, height, features), BF16),
        compiler_params=MOST_VMEM,
        name="outgoing_rows",
    )(gate, cot, mix, row_ids, own, other)


def dense_kernel(ids_ref, rows_ref, out_ref):
    tile, features = out_ref.shape
    lists, listed = ids_ref.shape
    row = (lax.broadcasted_iota(jnp.int32, (tile, listed), 0) + pl.program_id(0) * tile).astype(F32)
    total = jnp.zeros((tile, features), F32)
    together = 8
    for first in range(0, lists, together):
        hot = [
            jnp.where(row == ids_ref[pl.ds(k, 1), :], 1.0, 0.0).astype(BF16)
            for k in range(first, first + together)
        ]
        rows = [rows_ref[k, :listed, :] for k in range(first, first + together)]
        total += jnp.dot(
            jnp.concatenate(hot, axis=1), jnp.concatenate(rows, axis=0), preferred_element_type=F32
        )
    out_ref[...] = total.astype(BF16)


def dense_rows(ids, received, rows):
    lists, listed = ids.shape
    features = received.shape[-1]
    tile = 256
    return pl.pallas_call(
        dense_kernel,
        grid=(rows // tile,),
        in_specs=[
            pl.BlockSpec((lists, listed), lambda i: (0, 0)),
            pl.BlockSpec(received.shape, lambda i: (0, 0, 0)),
        ],
        out_specs=pl.BlockSpec((tile, features), lambda i: (i, 0)),
        out_shape=jax.ShapeDtypeStruct((rows, features), BF16),
        compiler_params=VMEM,
        cost_estimate=pl.CostEstimate(
            flops=2 * rows * lists * listed * features, bytes_accessed=received.size * 2, transcendentals=0
        ),
        name="dense_rows",
    )(ids, received)


def pick_kernel(ids_ref, place_ref, *refs):
    blocks, out_ref = refs[:-1], refs[-1]
    lists, listed = ids_ref.shape[1:]
    wanted = jnp.concatenate(
        [jnp.transpose(jnp.broadcast_to(ids_ref[0, k : k + 1, :], (128, listed))) for k in range(lists)],
        axis=0,
    )
    total = jnp.zeros(out_ref.shape[1:], F32)
    for b, block in enumerate(blocks):
        rows = block.shape[0]
        hot = [
            jnp.where(wanted == place_ref[b : b + 1, q : q + 128], 1.0, 0.0).astype(BF16)
            for q in range(0, rows, 128)
        ]
        total += jnp.dot(jnp.concatenate(hot, axis=1), block[...], preferred_element_type=F32)
    out_ref[0] = total.astype(BF16)


def picked_rows(ids, places, blocks):
    members, lists, listed = ids.shape
    rows, features = blocks[0].shape
    return pl.pallas_call(
        pick_kernel,
        grid=(members,),
        in_specs=[
            pl.BlockSpec((1, lists, listed), lambda i: (i, 0, 0)),
            pl.BlockSpec(places.shape, lambda i: (0, 0)),
        ]
        + [pl.BlockSpec((rows, features), lambda i: (0, 0))] * len(blocks),
        out_specs=pl.BlockSpec((1, lists * listed, features), lambda i: (i, 0, 0)),
        out_shape=jax.ShapeDtypeStruct((members, lists * listed, features), BF16),
        compiler_params=VMEM,
        cost_estimate=pl.CostEstimate(
            flops=2 * members * lists * listed * rows * len(blocks) * features,
            bytes_accessed=members * lists * listed * features * 2,
            transcendentals=0,
        ),
        name="picked_rows",
    )(ids, places, *blocks)


def final_kernel(
    rows_ref, mix_a_ref, mix_b_ref, gate_a_ref, cot_ref, gate_b_ref, slots_ref,
    mixed_ref, grad_gate_ref, grad_weights_ref, scores_ref,
):
    listed = mix_a_ref.shape[1]
    step, features = rows_ref.shape[0] // 2, rows_ref.shape[2] * 2

    @pl.when(pl.program_id(0) == 0)
    def _():
        scores_ref[...] = jnp.zeros_like(scores_ref)

    part = jnp.zeros(scores_ref.shape, F32)
    for k in range(step):
        at = slice(k * features, (k + 1) * features)
        fetched = jnp.concatenate([rows_ref[2 * k], rows_ref[2 * k + 1]], axis=1)
        fetched_a, fetched_b = fetched[:listed], fetched[listed:]
        memory_b = jnp.dot(mix_b_ref[...], fetched_b, preferred_element_type=F32)
        gb = gate_b_ref[0, :, at].astype(F32)
        mixed_ref[0, :, at] = (gb / (1.0 + jnp.exp(-gb)) * memory_b).astype(BF16)
        memory_a = jnp.dot(mix_a_ref[...], fetched_a, preferred_element_type=F32)
        g, sig, inc = gated(gate_a_ref[0, :, at], cot_ref[0, :, at])
        grad_gate_ref[0, :, at] = (inc * memory_a * sig * (1.0 + g * (1.0 - sig))).astype(BF16)
        grad_memory = (inc * g * sig).astype(BF16)
        part += lax.dot_general(
            grad_memory, fetched_a, (((1,), (1,)), ((), ())), preferred_element_type=F32
        )
    scores_ref[...] += part

    @pl.when(pl.program_id(0) == pl.num_programs(0) - 1)
    def _():
        grad_weights_ref[0] = jnp.take_along_axis(scores_ref[...], slots_ref[0, 0], axis=1)


def final_outputs(fetched, mix_a, mix_b, gate_a, cot, gate_b, slots):
    chunks, rows, features = fetched.shape
    _, tokens, width = gate_a.shape
    listed = mix_a.shape[1]
    step = 8
    whole = pl.BlockSpec((tokens, listed), lambda i: (0, 0))
    part = pl.BlockSpec((1, tokens, step * features), lambda i: (0, 0, i))
    return pl.pallas_call(
        final_kernel,
        grid=(chunks // step,),
        in_specs=[
            pl.BlockSpec((step, rows, features), lambda i: (i, 0, 0)),
            whole, whole, part, part, part,
            pl.BlockSpec((1, 1, tokens, listed), lambda i: (0, 0, 0, 0)),
        ],
        out_specs=[part, part, pl.BlockSpec((1, tokens, listed), lambda i: (0, 0, 0))],
        out_shape=[
            jax.ShapeDtypeStruct((1, tokens, width), BF16),
            jax.ShapeDtypeStruct((1, tokens, width), BF16),
            jax.ShapeDtypeStruct((1, tokens, listed), F32),
        ],
        scratch_shapes=[pltpu.VMEM((tokens, listed), F32)],
        compiler_params=VMEM,
        name="final_outputs",
    )(fetched, mix_a, mix_b, gate_a, cot, gate_b, slots)


def quarters(table):
    rows = table.shape[0] // 4
    zl0, core = lax.axis_index("zl0"), lax.axis_index("c")

    def quarter(z):
        return lax.dynamic_slice_in_dim(table, (z * 2 + core) * rows, rows, 0)

    mirrored = [(i, 7 - i) for i in range(8)]
    return quarter(zl0), lax.ppermute(quarter(1 - zl0), ("zl1", "zl0", "zh"), mirrored)


def from_pair(block, away):
    n_y = lax.axis_size(RING)
    return lax.ppermute(block, RING, [((i + 2 * away) % n_y, i) for i in range(n_y)])


def block_places(members, held):
    n_pairs = lax.axis_size("y1")
    pairs = (lax.axis_index("y1") + jnp.array((0,) + AWAY, jnp.int32)) & (n_pairs - 1)
    member = jnp.arange(members, dtype=jnp.int32)
    x = (member >> 4) * 2 + ((member >> 1) & 1)
    quarter, y_low = (member >> 2) & 3, member & 1
    zh = lax.axis_index("zh") ^ jnp.arange(2, dtype=jnp.int32)
    y = pairs[:, None] * 2 + y_low[None, :]
    holder = (x[None, :, None] * (2 * n_pairs) + y[:, :, None]) * 2 + zh[None, None, :]
    row = holder * ROWS_DEV + (quarter * held)[None, :, None]
    places = row[..., None] + jnp.arange(held, dtype=jnp.int32)
    return places.reshape(n_pairs, -1).astype(F32)


def local(gate_a, cotangent_a, gate_b, table, row_ids, slots, weights):
    rows_dev = table.shape[0]
    owners = lax.axis_size(TABLE)
    listed = row_ids.shape[-1]

    own, other = quarters(table)
    mix_a = mixing(slots, weights, 0)
    mix_a, other = lax.optimization_barrier((mix_a, other))
    sent = outgoing(gate_a, cotangent_a, mix_a, row_ids, own, other, 128)
    received = lax.all_to_all(sent, GROUP, split_axis=0, concat_axis=0, tiled=True)

    members, held = received.shape[0], own.shape[0]
    block = received[:, listed + 16 :].reshape(members * 2 * held, -1)
    codes = received[:, listed : listed + 4, :].astype(F32)
    ids = codes[:, 0::2] * ROWS_DEV + codes[:, 1::2]
    ids_a, rows = ids[:, 0], owners * rows_dev
    others = [from_pair(block, away) for away in AWAY]
    dense = dense_rows(ids_a, received, rows)
    dense, *others = lax.optimization_barrier((dense, *others))
    arrived = lax.all_to_all(
        dense.reshape(owners, rows_dev, -1), TABLE, split_axis=0, concat_axis=0, tiled=True
    )

    picked = picked_rows(ids, block_places(members, held), (block, *others))
    fetched = lax.all_to_all(picked, GROUP, split_axis=0, concat_axis=0, tiled=True)

    features = arrived.shape[-1]
    summed = jnp.sum(arrived.reshape(2, 2, -1, 2, 2, rows_dev, features).astype(F32), axis=(2, 4))
    mine = lax.axis_index("zl1")
    kept = lax.dynamic_index_in_dim(summed, mine, 0, keepdims=False)
    given = lax.dynamic_index_in_dim(summed, 1 - mine, 0, keepdims=False)
    total = kept + lax.ppermute(given, "zl1", [(0, 1), (1, 0)])
    grad_table = jnp.transpose(total, (2, 0, 1, 3)).reshape(rows_dev, -1)

    mixed, grad_gate, grad_weights = final_outputs(
        fetched, mix_a, mixing(slots, weights, 1), gate_a, cotangent_a, gate_b, slots
    )
    return mixed, grad_gate, grad_weights, grad_table


def solution(mesh):
    finer = Mesh(
        mesh.devices.reshape(2, 2, 2, 2, 2, 4, 2, 2),
        ("zl1", "zl0", "c", "x1", "x0", "y1", "y0", "zh"),
    )
    return jax.shard_map(
        local,
        mesh=finer,
        in_specs=(
            P(SECTION, TABLE, None),
            P(SECTION, TABLE, None),
            P(SECTION, TABLE, None),
            P(TABLE, None),
            P(SECTION, None, TABLE, None),
            P(SECTION, None, TABLE, None),
            P(SECTION, None, TABLE, None),
        ),
        out_specs=(
            P(SECTION, TABLE, None),
            P(SECTION, TABLE, None),
            P(SECTION, TABLE, None),
            P(TABLE, SECTION),
        ),
        check_vma=False,
    )
```

```python
import jax
import jax.numpy as jnp
from jax import lax
from jax.experimental import pallas as pl
from jax.experimental.pallas import tpu as pltpu
from jax.sharding import Mesh
from jax.sharding import PartitionSpec as P

SECTION = ("zl1", "zl0", "c")
TABLE = ("x1", "x0", "y1", "y0", "zh")
GROUP = ("x1", "zl0", "c", "x0", "y0")
RING = ("y1", "y0")
ROWS_DEV = 64
AWAY = (2, -1, 1)
F32 = jnp.float32
BF16 = jnp.bfloat16
VMEM = pltpu.CompilerParams(vmem_limit_bytes=40 * 1024 * 1024)
MOST_VMEM = pltpu.CompilerParams(vmem_limit_bytes=60 * 1024 * 1024)


def gated(gate, incoming):
    g = gate.astype(F32)
    sig = 1.0 / (1.0 + jnp.exp(-g))
    return g, sig, incoming.astype(F32)


def mixing_of(slots, weights):
    position = lax.broadcasted_iota(jnp.int32, slots.shape, 1)
    total = jnp.zeros(slots.shape, F32)
    for p in range(slots.shape[1]):
        total += jnp.where(slots[:, p : p + 1] == position, weights[:, p : p + 1], 0.0)
    return total.astype(BF16)


def mixing_kernel(slots_ref, weights_ref, out_ref):
    out_ref[...] = mixing_of(slots_ref[0, 0], weights_ref[0, 0])


def mixing(slots, weights, batch, limit):
    tokens, listed = slots.shape[2:]
    picks = pl.BlockSpec((1, 1, tokens, listed), lambda i: (0, batch, 0, 0))
    return pl.pallas_call(
        mixing_kernel,
        grid=(1,),
        in_specs=[picks, picks],
        out_specs=pl.BlockSpec((tokens, listed), lambda i: (0, 0)),
        out_shape=jax.ShapeDtypeStruct((tokens, listed), BF16),
        compiler_params=limit,
        name="mixing",
    )(slots, weights)


def outgoing_kernel(gate_ref, cot_ref, mix_ref, ids_ref, out_ref):
    listed = mix_ref.shape[1]
    g, sig, inc = gated(gate_ref[0], cot_ref[0])
    grad_memory = (inc * g * sig).astype(BF16)
    rows = lax.dot_general(
        mix_ref[...], grad_memory, (((0,), (0,)), ((), ())), preferred_element_type=F32
    ).astype(BF16)
    ids = [ids_ref[0, c] for c in range(2)]
    codes = jnp.concatenate(
        [part for i in ids for part in (i // ROWS_DEV, i % ROWS_DEV)] + [jnp.zeros((12, listed), jnp.int32)]
    )
    codes = codes.astype(F32).astype(BF16)
    for k in range(out_ref.shape[0]):
        out_ref[k, :listed, :] = rows[:, k * 128 : (k + 1) * 128]
        out_ref[k, listed:, :] = codes


def outgoing(gate, cot, mix, row_ids, height, features):
    _, tokens, width = gate.shape
    listed = row_ids.shape[-1]
    chunks, step = width // features, 8
    part = pl.BlockSpec((1, tokens, step * features), lambda i: (0, 0, i))
    return pl.pallas_call(
        outgoing_kernel,
        grid=(chunks // step,),
        in_specs=[
            part, part,
            pl.BlockSpec((tokens, listed), lambda i: (0, 0)),
            pl.BlockSpec(row_ids.shape, lambda i: (0, 0, 0, 0)),
        ],
        out_specs=pl.BlockSpec((step, listed + 16, features), lambda i: (i, 0, 0)),
        out_shape=jax.ShapeDtypeStruct((chunks, height, features), BF16),
        compiler_params=MOST_VMEM,
        name="outgoing_rows",
    )(gate, cot, mix, row_ids)


def table_rows_kernel(own_ref, other_ref, payload_ref, out_ref):
    features = out_ref.shape[2]

    def put(rows_ref):
        for k in range(out_ref.shape[0]):
            out_ref[k] = rows_ref[:, k * features : (k + 1) * features]

    @pl.when(pl.program_id(0) == 0)
    def _():
        put(own_ref)

    @pl.when(pl.program_id(0) == 1)
    def _():
        put(other_ref)


def with_table_rows(payload, own, other):
    chunks, height, features = payload.shape
    held, width = own.shape
    at = height // held - 2
    rows = pl.BlockSpec((held, width), lambda i: (0, 0))
    return pl.pallas_call(
        table_rows_kernel,
        grid=(2,),
        in_specs=[rows, rows, pl.BlockSpec(memory_space=pl.ANY)],
        out_specs=pl.BlockSpec((chunks, held, features), lambda i: (0, at + i, 0)),
        out_shape=jax.ShapeDtypeStruct(payload.shape, BF16),
        input_output_aliases={2: 0},
        compiler_params=MOST_VMEM,
        name="table_rows",
    )(own, other, payload)


def dense_kernel(ids_ref, rows_ref, out_ref):
    tile, features = out_ref.shape
    lists, listed = ids_ref.shape
    row = (lax.broadcasted_iota(jnp.int32, (tile, listed), 0) + pl.program_id(0) * tile).astype(F32)
    total = jnp.zeros((tile, features), F32)
    together = 8
    for first in range(0, lists, together):
        hot = [
            jnp.where(row == ids_ref[pl.ds(k, 1), :], 1.0, 0.0).astype(BF16)
            for k in range(first, first + together)
        ]
        rows = [rows_ref[k, :listed, :] for k in range(first, first + together)]
        total += jnp.dot(
            jnp.concatenate(hot, axis=1), jnp.concatenate(rows, axis=0), preferred_element_type=F32
        )
    out_ref[...] = total.astype(BF16)


def dense_rows(ids, received, rows):
    lists, listed = ids.shape
    features = received.shape[-1]
    tile = 256
    return pl.pallas_call(
        dense_kernel,
        grid=(rows // tile,),
        in_specs=[
            pl.BlockSpec((lists, listed), lambda i: (0, 0)),
            pl.BlockSpec(received.shape, lambda i: (0, 0, 0)),
        ],
        out_specs=pl.BlockSpec((tile, features), lambda i: (i, 0)),
        out_shape=jax.ShapeDtypeStruct((rows, features), BF16),
        compiler_params=VMEM,
        cost_estimate=pl.CostEstimate(
            flops=2 * rows * lists * listed * features, bytes_accessed=received.size * 2, transcendentals=0
        ),
        name="dense_rows",
    )(ids, received)


def pick_kernel(ids_ref, place_ref, *refs):
    blocks, out_ref = refs[:-1], refs[-1]
    lists, listed = ids_ref.shape[1:]
    wanted = jnp.concatenate(
        [jnp.transpose(jnp.broadcast_to(ids_ref[0, k : k + 1, :], (128, listed))) for k in range(lists)],
        axis=0,
    )
    total = jnp.zeros(out_ref.shape[1:], F32)
    for b, block in enumerate(blocks):
        rows = block.shape[0]
        hot = [
            jnp.where(wanted == place_ref[b : b + 1, q : q + 128], 1.0, 0.0).astype(BF16)
            for q in range(0, rows, 128)
        ]
        total += jnp.dot(jnp.concatenate(hot, axis=1), block[...], preferred_element_type=F32)
    out_ref[0] = total.astype(BF16)


def picked_rows(ids, places, blocks):
    members, lists, listed = ids.shape
    rows, features = blocks[0].shape
    return pl.pallas_call(
        pick_kernel,
        grid=(members,),
        in_specs=[
            pl.BlockSpec((1, lists, listed), lambda i: (i, 0, 0)),
            pl.BlockSpec(places.shape, lambda i: (0, 0)),
        ]
        + [pl.BlockSpec((rows, features), lambda i: (0, 0))] * len(blocks),
        out_specs=pl.BlockSpec((1, lists * listed, features), lambda i: (i, 0, 0)),
        out_shape=jax.ShapeDtypeStruct((members, lists * listed, features), BF16),
        compiler_params=VMEM,
        cost_estimate=pl.CostEstimate(
            flops=2 * members * lists * listed * rows * len(blocks) * features,
            bytes_accessed=members * lists * listed * features * 2,
            transcendentals=0,
        ),
        name="picked_rows",
    )(ids, places, *blocks)


def final_kernel(
    rows_ref, mix_a_ref, mix_b_ref, gate_a_ref, cot_ref, gate_b_ref, slots_ref,
    mixed_ref, grad_gate_ref, grad_weights_ref, scores_ref,
):
    listed = mix_a_ref.shape[1]
    step, features = rows_ref.shape[0] // 2, rows_ref.shape[2] * 2

    @pl.when(pl.program_id(0) == 0)
    def _():
        scores_ref[...] = jnp.zeros_like(scores_ref)

    part = jnp.zeros(scores_ref.shape, F32)
    for k in range(step):
        at = slice(k * features, (k + 1) * features)
        fetched = jnp.concatenate([rows_ref[2 * k], rows_ref[2 * k + 1]], axis=1)
        fetched_a, fetched_b = fetched[:listed], fetched[listed:]
        memory_b = jnp.dot(mix_b_ref[...], fetched_b, preferred_element_type=F32)
        gb = gate_b_ref[0, :, at].astype(F32)
        mixed_ref[0, :, at] = (gb / (1.0 + jnp.exp(-gb)) * memory_b).astype(BF16)
        memory_a = jnp.dot(mix_a_ref[...], fetched_a, preferred_element_type=F32)
        g, sig, inc = gated(gate_a_ref[0, :, at], cot_ref[0, :, at])
        grad_gate_ref[0, :, at] = (inc * memory_a * sig * (1.0 + g * (1.0 - sig))).astype(BF16)
        grad_memory = (inc * g * sig).astype(BF16)
        part += lax.dot_general(
            grad_memory, fetched_a, (((1,), (1,)), ((), ())), preferred_element_type=F32
        )
    scores_ref[...] += part

    @pl.when(pl.program_id(0) == pl.num_programs(0) - 1)
    def _():
        grad_weights_ref[0] = jnp.take_along_axis(scores_ref[...], slots_ref[0, 0], axis=1)


def final_outputs(fetched, mix_a, mix_b, gate_a, cot, gate_b, slots):
    chunks, rows, features = fetched.shape
    _, tokens, width = gate_a.shape
    listed = mix_a.shape[1]
    step = 8
    whole = pl.BlockSpec((tokens, listed), lambda i: (0, 0))
    part = pl.BlockSpec((1, tokens, step * features), lambda i: (0, 0, i))
    return pl.pallas_call(
        final_kernel,
        grid=(chunks // step,),
        in_specs=[
            pl.BlockSpec((step, rows, features), lambda i: (i, 0, 0)),
            whole, whole, part, part, part,
            pl.BlockSpec((1, 1, tokens, listed), lambda i: (0, 0, 0, 0)),
        ],
        out_specs=[part, part, pl.BlockSpec((1, tokens, listed), lambda i: (0, 0, 0))],
        out_shape=[
            jax.ShapeDtypeStruct((1, tokens, width), BF16),
            jax.ShapeDtypeStruct((1, tokens, width), BF16),
            jax.ShapeDtypeStruct((1, tokens, listed), F32),
        ],
        scratch_shapes=[pltpu.VMEM((tokens, listed), F32)],
        compiler_params=VMEM,
        name="final_outputs",
    )(fetched, mix_a, mix_b, gate_a, cot, gate_b, slots)


def quarters(table):
    rows = table.shape[0] // 4
    zl0, core = lax.axis_index("zl0"), lax.axis_index("c")

    def quarter(z):
        return lax.dynamic_slice_in_dim(table, (z * 2 + core) * rows, rows, 0)

    mirrored = [(i, 7 - i) for i in range(8)]
    return quarter(zl0), lax.ppermute(quarter(1 - zl0), ("zl1", "zl0", "zh"), mirrored)


def from_pair(block, away):
    n_y = lax.axis_size(RING)
    return lax.ppermute(block, RING, [((i + 2 * away) % n_y, i) for i in range(n_y)])


def block_places(members, held):
    n_pairs = lax.axis_size("y1")
    pairs = (lax.axis_index("y1") + jnp.array((0,) + AWAY, jnp.int32)) & (n_pairs - 1)
    member = jnp.arange(members, dtype=jnp.int32)
    x = (member >> 4) * 2 + ((member >> 1) & 1)
    quarter, y_low = (member >> 2) & 3, member & 1
    zh = lax.axis_index("zh") ^ jnp.arange(2, dtype=jnp.int32)
    y = pairs[:, None] * 2 + y_low[None, :]
    holder = (x[None, :, None] * (2 * n_pairs) + y[:, :, None]) * 2 + zh[None, None, :]
    row = holder * ROWS_DEV + (quarter * held)[None, :, None]
    places = row[..., None] + jnp.arange(held, dtype=jnp.int32)
    return places.reshape(n_pairs, -1).astype(F32)


def local(gate_a, cotangent_a, gate_b, table, row_ids, slots, weights):
    rows_dev = table.shape[0]
    owners = lax.axis_size(TABLE)
    listed = row_ids.shape[-1]

    own, other = quarters(table)
    held = own.shape[0]
    mix_a = mixing(slots, weights, 0, MOST_VMEM)
    sent = outgoing(gate_a, cotangent_a, mix_a, row_ids, listed + 16 + 2 * held, 128)
    sent, other = lax.optimization_barrier((sent, other))
    sent = with_table_rows(sent, own, other)
    received = lax.all_to_all(sent, GROUP, split_axis=0, concat_axis=0, tiled=True)

    members = received.shape[0]
    block = received[:, listed + 16 :].reshape(members * 2 * held, -1)
    codes = received[:, listed : listed + 4, :].astype(F32)
    ids = codes[:, 0::2] * ROWS_DEV + codes[:, 1::2]
    ids_a, rows = ids[:, 0], owners * rows_dev
    others = [from_pair(block, away) for away in AWAY]
    dense = dense_rows(ids_a, received, rows)
    dense, *others = lax.optimization_barrier((dense, *others))
    arrived = lax.all_to_all(
        dense.reshape(owners, rows_dev, -1), TABLE, split_axis=0, concat_axis=0, tiled=True
    )

    picked = picked_rows(ids, block_places(members, held), (block, *others))
    fetched = lax.all_to_all(picked, GROUP, split_axis=0, concat_axis=0, tiled=True)

    features = arrived.shape[-1]
    summed = jnp.sum(arrived.reshape(2, 2, -1, 2, 2, rows_dev, features).astype(F32), axis=(2, 4))
    mine = lax.axis_index("zl1")
    kept = lax.dynamic_index_in_dim(summed, mine, 0, keepdims=False)
    given = lax.dynamic_index_in_dim(summed, 1 - mine, 0, keepdims=False)
    total = kept + lax.ppermute(given, "zl1", [(0, 1), (1, 0)])
    grad_table = jnp.transpose(total, (2, 0, 1, 3)).reshape(rows_dev, -1)

    mixed, grad_gate, grad_weights = final_outputs(
        fetched, mix_a, mixing(slots, weights, 1, VMEM), gate_a, cotangent_a, gate_b, slots
    )
    return mixed, grad_gate, grad_weights, grad_table


def solution(mesh):
    finer = Mesh(
        mesh.devices.reshape(2, 2, 2, 2, 2, 4, 2, 2),
        ("zl1", "zl0", "c", "x1", "x0", "y1", "y0", "zh"),
    )
    return jax.shard_map(
        local,
        mesh=finer,
        in_specs=(
            P(SECTION, TABLE, None),
            P(SECTION, TABLE, None),
            P(SECTION, TABLE, None),
            P(TABLE, None),
            P(SECTION, None, TABLE, None),
            P(SECTION, None, TABLE, None),
            P(SECTION, None, TABLE, None),
        ),
        out_specs=(
            P(SECTION, TABLE, None),
            P(SECTION, TABLE, None),
            P(SECTION, TABLE, None),
            P(TABLE, SECTION),
        ),
        check_vma=False,
    )
```

```python
import jax
import jax.numpy as jnp
from jax import lax
from jax.experimental import pallas as pl
from jax.experimental.pallas import tpu as pltpu
from jax.sharding import Mesh
from jax.sharding import PartitionSpec as P

SECTION = ("zl1", "zl0", "c")
TABLE = ("x1", "x0", "y1", "y0", "zh")
GROUP = ("x1", "zl0", "c", "x0", "y0")
RING = ("y1", "y0")
ROWS_DEV = 64
AWAY = (-1, 1, 2)
F32 = jnp.float32
BF16 = jnp.bfloat16
VMEM = pltpu.CompilerParams(vmem_limit_bytes=40 * 1024 * 1024)
MOST_VMEM = pltpu.CompilerParams(vmem_limit_bytes=60 * 1024 * 1024)


def gated(gate, incoming):
    g = gate.astype(F32)
    sig = 1.0 / (1.0 + jnp.exp(-g))
    return g, sig, incoming.astype(F32)


def mixing_of(slots, weights):
    position = lax.broadcasted_iota(jnp.int32, slots.shape, 1)
    total = jnp.zeros(slots.shape, F32)
    for p in range(slots.shape[1]):
        total += jnp.where(slots[:, p : p + 1] == position, weights[:, p : p + 1], 0.0)
    return total.astype(BF16)


def mixing_kernel(slots_ref, weights_ref, out_ref):
    out_ref[...] = mixing_of(slots_ref[0, 0], weights_ref[0, 0])


def mixing(slots, weights, batch, limit):
    tokens, listed = slots.shape[2:]
    picks = pl.BlockSpec((1, 1, tokens, listed), lambda i: (0, batch, 0, 0))
    return pl.pallas_call(
        mixing_kernel,
        grid=(1,),
        in_specs=[picks, picks],
        out_specs=pl.BlockSpec((tokens, listed), lambda i: (0, 0)),
        out_shape=jax.ShapeDtypeStruct((tokens, listed), BF16),
        compiler_params=limit,
        name="mixing",
    )(slots, weights)


def outgoing_kernel(gate_ref, cot_ref, mix_ref, ids_ref, out_ref):
    listed = mix_ref.shape[1]
    g, sig, inc = gated(gate_ref[0], cot_ref[0])
    grad_memory = (inc * g * sig).astype(BF16)
    rows = lax.dot_general(
        mix_ref[...], grad_memory, (((0,), (0,)), ((), ())), preferred_element_type=F32
    ).astype(BF16)
    ids = [ids_ref[0, c] for c in range(2)]
    codes = jnp.concatenate(
        [part for i in ids for part in (i // ROWS_DEV, i % ROWS_DEV)] + [jnp.zeros((12, listed), jnp.int32)]
    )
    codes = codes.astype(F32).astype(BF16)
    for k in range(out_ref.shape[0]):
        out_ref[k, :listed, :] = rows[:, k * 128 : (k + 1) * 128]
        out_ref[k, listed:, :] = codes


def outgoing(gate, cot, mix, row_ids, height, features):
    _, tokens, width = gate.shape
    listed = row_ids.shape[-1]
    chunks, step = width // features, 8
    part = pl.BlockSpec((1, tokens, step * features), lambda i: (0, 0, i))
    return pl.pallas_call(
        outgoing_kernel,
        grid=(chunks // step,),
        in_specs=[
            part, part,
            pl.BlockSpec((tokens, listed), lambda i: (0, 0)),
            pl.BlockSpec(row_ids.shape, lambda i: (0, 0, 0, 0)),
        ],
        out_specs=pl.BlockSpec((step, listed + 16, features), lambda i: (i, 0, 0)),
        out_shape=jax.ShapeDtypeStruct((chunks, height, features), BF16),
        compiler_params=MOST_VMEM,
        name="outgoing_rows",
    )(gate, cot, mix, row_ids)


def table_rows_kernel(own_ref, other_ref, payload_ref, out_ref):
    features = out_ref.shape[2]

    def put(rows_ref):
        for k in range(out_ref.shape[0]):
            out_ref[k] = rows_ref[:, k * features : (k + 1) * features]

    @pl.when(pl.program_id(0) == 0)
    def _():
        put(own_ref)

    @pl.when(pl.program_id(0) == 1)
    def _():
        put(other_ref)


def with_table_rows(payload, own, other):
    chunks, height, features = payload.shape
    held, width = own.shape
    at = height // held - 2
    rows = pl.BlockSpec((held, width), lambda i: (0, 0))
    return pl.pallas_call(
        table_rows_kernel,
        grid=(2,),
        in_specs=[rows, rows, pl.BlockSpec(memory_space=pl.ANY)],
        out_specs=pl.BlockSpec((chunks, held, features), lambda i: (0, at + i, 0)),
        out_shape=jax.ShapeDtypeStruct(payload.shape, BF16),
        input_output_aliases={2: 0},
        compiler_params=MOST_VMEM,
        name="table_rows",
    )(own, other, payload)


def dense_kernel(ids_ref, rows_ref, out_ref):
    tile, features = out_ref.shape
    lists, listed = ids_ref.shape
    row = (lax.broadcasted_iota(jnp.int32, (tile, listed), 0) + pl.program_id(0) * tile).astype(F32)
    total = jnp.zeros((tile, features), F32)
    together = 8
    for first in range(0, lists, together):
        hot = [
            jnp.where(row == ids_ref[pl.ds(k, 1), :], 1.0, 0.0).astype(BF16)
            for k in range(first, first + together)
        ]
        rows = [rows_ref[k, :listed, :] for k in range(first, first + together)]
        total += jnp.dot(
            jnp.concatenate(hot, axis=1), jnp.concatenate(rows, axis=0), preferred_element_type=F32
        )
    out_ref[...] = total.astype(BF16)


def dense_rows(ids, received, rows):
    lists, listed = ids.shape
    features = received.shape[-1]
    tile = 256
    return pl.pallas_call(
        dense_kernel,
        grid=(rows // tile,),
        in_specs=[
            pl.BlockSpec((lists, listed), lambda i: (0, 0)),
            pl.BlockSpec(received.shape, lambda i: (0, 0, 0)),
        ],
        out_specs=pl.BlockSpec((tile, features), lambda i: (i, 0)),
        out_shape=jax.ShapeDtypeStruct((rows, features), BF16),
        compiler_params=VMEM,
        cost_estimate=pl.CostEstimate(
            flops=2 * rows * lists * listed * features, bytes_accessed=received.size * 2, transcendentals=0
        ),
        name="dense_rows",
    )(ids, received)


def pick_kernel(ids_ref, place_ref, *refs):
    blocks, out_ref = refs[:-1], refs[-1]
    lists, listed = ids_ref.shape[1:]
    wanted = jnp.concatenate(
        [jnp.transpose(jnp.broadcast_to(ids_ref[0, k : k + 1, :], (128, listed))) for k in range(lists)],
        axis=0,
    )
    total = jnp.zeros(out_ref.shape[1:], F32)
    for b, block in enumerate(blocks):
        rows = block.shape[0]
        hot = [
            jnp.where(wanted == place_ref[b : b + 1, q : q + 128], 1.0, 0.0).astype(BF16)
            for q in range(0, rows, 128)
        ]
        total += jnp.dot(jnp.concatenate(hot, axis=1), block[...], preferred_element_type=F32)
    out_ref[0] = total.astype(BF16)


def picked_rows(ids, places, blocks):
    members, lists, listed = ids.shape
    rows, features = blocks[0].shape
    return pl.pallas_call(
        pick_kernel,
        grid=(members,),
        in_specs=[
            pl.BlockSpec((1, lists, listed), lambda i: (i, 0, 0)),
            pl.BlockSpec(places.shape, lambda i: (0, 0)),
        ]
        + [pl.BlockSpec((rows, features), lambda i: (0, 0))] * len(blocks),
        out_specs=pl.BlockSpec((1, lists * listed, features), lambda i: (i, 0, 0)),
        out_shape=jax.ShapeDtypeStruct((members, lists * listed, features), BF16),
        compiler_params=VMEM,
        cost_estimate=pl.CostEstimate(
            flops=2 * members * lists * listed * rows * len(blocks) * features,
            bytes_accessed=members * lists * listed * features * 2,
            transcendentals=0,
        ),
        name="picked_rows",
    )(ids, places, *blocks)


def final_kernel(
    rows_ref, mix_a_ref, mix_b_ref, gate_a_ref, cot_ref, gate_b_ref, slots_ref,
    mixed_ref, grad_gate_ref, grad_weights_ref, scores_ref,
):
    listed = mix_a_ref.shape[1]
    step, features = rows_ref.shape[0] // 2, rows_ref.shape[2] * 2

    @pl.when(pl.program_id(0) == 0)
    def _():
        scores_ref[...] = jnp.zeros_like(scores_ref)

    part = jnp.zeros(scores_ref.shape, F32)
    for k in range(step):
        at = slice(k * features, (k + 1) * features)
        fetched = jnp.concatenate([rows_ref[2 * k], rows_ref[2 * k + 1]], axis=1)
        fetched_a, fetched_b = fetched[:listed], fetched[listed:]
        memory_b = jnp.dot(mix_b_ref[...], fetched_b, preferred_element_type=F32)
        gb = gate_b_ref[0, :, at].astype(F32)
        mixed_ref[0, :, at] = (gb / (1.0 + jnp.exp(-gb)) * memory_b).astype(BF16)
        memory_a = jnp.dot(mix_a_ref[...], fetched_a, preferred_element_type=F32)
        g, sig, inc = gated(gate_a_ref[0, :, at], cot_ref[0, :, at])
        grad_gate_ref[0, :, at] = (inc * memory_a * sig * (1.0 + g * (1.0 - sig))).astype(BF16)
        grad_memory = (inc * g * sig).astype(BF16)
        part += lax.dot_general(
            grad_memory, fetched_a, (((1,), (1,)), ((), ())), preferred_element_type=F32
        )
    scores_ref[...] += part

    @pl.when(pl.program_id(0) == pl.num_programs(0) - 1)
    def _():
        grad_weights_ref[0] = jnp.take_along_axis(scores_ref[...], slots_ref[0, 0], axis=1)


def final_outputs(fetched, mix_a, mix_b, gate_a, cot, gate_b, slots):
    chunks, rows, features = fetched.shape
    _, tokens, width = gate_a.shape
    listed = mix_a.shape[1]
    step = 8
    whole = pl.BlockSpec((tokens, listed), lambda i: (0, 0))
    part = pl.BlockSpec((1, tokens, step * features), lambda i: (0, 0, i))
    return pl.pallas_call(
        final_kernel,
        grid=(chunks // step,),
        in_specs=[
            pl.BlockSpec((step, rows, features), lambda i: (i, 0, 0)),
            whole, whole, part, part, part,
            pl.BlockSpec((1, 1, tokens, listed), lambda i: (0, 0, 0, 0)),
        ],
        out_specs=[part, part, pl.BlockSpec((1, tokens, listed), lambda i: (0, 0, 0))],
        out_shape=[
            jax.ShapeDtypeStruct((1, tokens, width), BF16),
            jax.ShapeDtypeStruct((1, tokens, width), BF16),
            jax.ShapeDtypeStruct((1, tokens, listed), F32),
        ],
        scratch_shapes=[pltpu.VMEM((tokens, listed), F32)],
        compiler_params=VMEM,
        name="final_outputs",
    )(fetched, mix_a, mix_b, gate_a, cot, gate_b, slots)


def quarters(table):
    rows = table.shape[0] // 4
    zl0, core = lax.axis_index("zl0"), lax.axis_index("c")

    def quarter(z):
        return lax.dynamic_slice_in_dim(table, (z * 2 + core) * rows, rows, 0)

    mirrored = [(i, 7 - i) for i in range(8)]
    return quarter(zl0), lax.ppermute(quarter(1 - zl0), ("zl1", "zl0", "zh"), mirrored)


def from_pair(block, away):
    n_y = lax.axis_size(RING)
    return lax.ppermute(block, RING, [((i + 2 * away) % n_y, i) for i in range(n_y)])


def block_places(members, held):
    n_pairs = lax.axis_size("y1")
    pairs = (lax.axis_index("y1") + jnp.array((0,) + AWAY, jnp.int32)) & (n_pairs - 1)
    member = jnp.arange(members, dtype=jnp.int32)
    x = (member >> 4) * 2 + ((member >> 1) & 1)
    quarter, y_low = (member >> 2) & 3, member & 1
    zh = lax.axis_index("zh") ^ jnp.arange(2, dtype=jnp.int32)
    y = pairs[:, None] * 2 + y_low[None, :]
    holder = (x[None, :, None] * (2 * n_pairs) + y[:, :, None]) * 2 + zh[None, None, :]
    row = holder * ROWS_DEV + (quarter * held)[None, :, None]
    places = row[..., None] + jnp.arange(held, dtype=jnp.int32)
    return places.reshape(n_pairs, -1).astype(F32)


def local(gate_a, cotangent_a, gate_b, table, row_ids, slots, weights):
    rows_dev = table.shape[0]
    owners = lax.axis_size(TABLE)
    listed = row_ids.shape[-1]

    own, other = quarters(table)
    held = own.shape[0]
    mix_a = mixing(slots, weights, 0, MOST_VMEM)
    sent = outgoing(gate_a, cotangent_a, mix_a, row_ids, listed + 16 + 2 * held, 128)
    sent, other = lax.optimization_barrier((sent, other))
    sent = with_table_rows(sent, own, other)
    received = lax.all_to_all(sent, GROUP, split_axis=0, concat_axis=0, tiled=True)

    members = received.shape[0]
    block = received[:, listed + 16 :].reshape(members * 2 * held, -1)
    codes = received[:, listed : listed + 4, :].astype(F32)
    ids = codes[:, 0::2] * ROWS_DEV + codes[:, 1::2]
    ids_a, rows = ids[:, 0], owners * rows_dev
    others = [from_pair(block, away) for away in AWAY]
    dense = dense_rows(ids_a, received, rows)
    dense, *others = lax.optimization_barrier((dense, *others))
    arrived = lax.all_to_all(
        dense.reshape(owners, rows_dev, -1), TABLE, split_axis=0, concat_axis=0, tiled=True
    )

    picked = picked_rows(ids, block_places(members, held), (block, *others))
    fetched = lax.all_to_all(picked, GROUP, split_axis=0, concat_axis=0, tiled=True)

    features = arrived.shape[-1]
    summed = jnp.sum(arrived.reshape(2, 2, -1, 2, 2, rows_dev, features).astype(F32), axis=(2, 4))
    mine = lax.axis_index("zl1")
    kept = lax.dynamic_index_in_dim(summed, mine, 0, keepdims=False)
    given = lax.dynamic_index_in_dim(summed, 1 - mine, 0, keepdims=False)
    total = kept + lax.ppermute(given.astype(BF16), "zl1", [(0, 1), (1, 0)]).astype(F32)
    grad_table = jnp.transpose(total, (2, 0, 1, 3)).reshape(rows_dev, -1)

    mixed, grad_gate, grad_weights = final_outputs(
        fetched, mix_a, mixing(slots, weights, 1, VMEM), gate_a, cotangent_a, gate_b, slots
    )
    return mixed, grad_gate, grad_weights, grad_table


def solution(mesh):
    finer = Mesh(
        mesh.devices.reshape(2, 2, 2, 2, 2, 4, 2, 2),
        ("zl1", "zl0", "c", "x1", "x0", "y1", "y0", "zh"),
    )
    return jax.shard_map(
        local,
        mesh=finer,
        in_specs=(
            P(SECTION, TABLE, None),
            P(SECTION, TABLE, None),
            P(SECTION, TABLE, None),
            P(TABLE, None),
            P(SECTION, None, TABLE, None),
            P(SECTION, None, TABLE, None),
            P(SECTION, None, TABLE, None),
        ),
        out_specs=(
            P(SECTION, TABLE, None),
            P(SECTION, TABLE, None),
            P(SECTION, TABLE, None),
            P(TABLE, SECTION),
        ),
        check_vma=False,
    )
```
